1024 devices in a mesh: slab: 32 (over z), chan: 16 (over x_hi, y, core), pipe: 2 (over x_lo).
Axes of the slice: x: 4 (x_hi: 2, x_lo: 2; x = x_hi * 2 + x_lo), y: 4, z: 32, core: 2. Of those that a mesh axis runs over, the one named last changes fastest.
Arguments:
- features: bfloat16 [2, 3, 64, 512, 128], P('pipe', None, 'slab', 'chan'), may hold values from -6 to 6
- taps: bfloat16 [2, 3, 512], P('pipe', None, 'chan'), may hold values from -3 to 3
- kern: bfloat16 [2, 512, 9, 512], P('pipe'), may hold values from -0.09375 to 0.09375
- proj: bfloat16 [2, 512, 16], P('pipe'), may hold values from -0.5 to 0.5
Outputs:
- section_out: bfloat16 [2, 3, 64, 512, 128], P('pipe', None, 'slab', 'chan')
- conv_grad: float32 [2, 512, 9, 512], P('pipe', 'slab', None, 'chan')
The draws below stay inside these ranges and needn't reach their ends.
All inputs are finite; a program needn't handle non-finite values.
Results may differ from the reference program's by a relative error of at most 0.015.
Values may be sent and summed in bfloat16 or wider, within the bound.
No kernel may reach another device: no remote copies, remote signals or barrier semaphores. Data moves between devices by JAX's collectives and lax.ppermute only.
A program may use at most 32 MiB of HBM per device.

```python
import math
import jax
import jax.numpy as jnp

C = 512
L = 16
FRAMES = 3
WIDTH = 128
ROWS = 64
SECTIONS = 2


def raised(entries, key, source, target, parts, factor):
    def block_of(axis_at):
        return (jnp.arange(entries.shape[axis_at]) // (entries.shape[axis_at] // parts)).reshape((-1,) + (1,) * (entries.ndim - 1 - axis_at))

    near = jax.random.permutation(key, parts)[block_of(target)]
    second = (block_of(target) + parts // 2) % parts
    return jnp.where((block_of(source) == near) | (block_of(source) == second), factor * entries, entries)


def level_of(key, shape, shards, low, top_value):
    loudness, own = 1.0, jax.random.fold_in(key, 6)
    for dim, blocks in shards:
        draws = jnp.exp(jax.random.uniform(jax.random.fold_in(own, dim), (blocks,), jnp.float32, low / len(shards), top_value / len(shards)))
        loudness = loudness * jnp.repeat(draws, shape[dim] // blocks).reshape([-1 if axis == dim else 1 for axis in range(len(shape))])
    return loudness


def normal_values(own_key, extent, width, most, split=(), dtype=jnp.bfloat16):
    loudness = level_of(own_key, extent, split, -0.22, 0.18) if split else 1.0
    drawn = jax.random.normal(own_key, extent, jnp.float32) * width * loudness
    return jnp.minimum(jnp.maximum(drawn, -most), most).astype(dtype)


def gaussian_with(own_key, dims, deviation, most, cuts, heavy, dtype=jnp.bfloat16):
    entries = deviation * jax.random.normal(own_key, dims, jnp.float32)
    if cuts:
        entries = entries * level_of(own_key, dims, cuts, -0.22, 0.18)
    return jnp.clip(raised(entries, jax.random.fold_in(own_key, 3), *heavy), -most, most).astype(dtype)


def setup_inputs(seed: int = 0) -> dict:
    keys = jax.random.split(jax.random.key(seed), 5)
    return {
        "features": gaussian_with(keys[0], (SECTIONS, FRAMES, ROWS, C, WIDTH), 1.0, 6.0, ((0, 2), (2, 32), (3, 16)), (2, 3, 32, 2.75)),
        "taps": normal_values(keys[1], (SECTIONS, 3, C), 0.6, 3.0, ((0, 2), (2, 16))),
        "kern": normal_values(keys[2], (SECTIONS, C, 9, C), (9 * C) ** -0.5, 0.09375, ((0, 2),)),
        "proj": normal_values(keys[3], (SECTIONS, C, L), (C // 4) ** -0.5, 0.5, ((0, 2),)),
    }


def squash(summed):
    sigma = jax.nn.sigmoid(summed)
    return sigma * (1.0 + summed * (1.0 - sigma))

def delayed(values, lag):
    padded = jnp.pad(values, ((lag, 0), (0, 0), (0, 0), (0, 0)))
    return padded[:values.shape[0]]

def advanced(values, lag):
    padded = jnp.pad(values, ((0, lag), (0, 0), (0, 0), (0, 0)))
    return padded[lag:]

def temporal(inputs, depth_taps):
    total = depth_taps[0][None, None, :, None] * inputs
    total = total + depth_taps[1][None, None, :, None] * delayed(inputs, 1)
    total = total + depth_taps[2][None, None, :, None] * delayed(inputs, 2)
    return total

def convolve(mixed, kernel):
    tile_rows = mixed.shape[1]
    columns = mixed.shape[3]
    padded = jnp.pad(mixed.astype(jnp.float32), ((0, 0), (1, 1), (0, 0), (1, 1)))
    total = jnp.zeros((mixed.shape[0], tile_rows, kernel.shape[2], columns), jnp.float32)
    for row_tap in range(3):
        for col_tap in range(3):
            window = padded[:, row_tap:row_tap + tile_rows, :, col_tap:col_tap + columns]
            total = total + jnp.einsum('frcw,co->frow', window, kernel[:, 3 * row_tap + col_tap, :].astype(jnp.float32))
    return total

def adjoint(grad_sum, kernel):
    tile_rows = grad_sum.shape[1]
    columns = grad_sum.shape[3]
    padded = jnp.pad(grad_sum.astype(jnp.float32), ((0, 0), (1, 1), (0, 0), (1, 1)))
    total = jnp.zeros((grad_sum.shape[0], tile_rows, kernel.shape[0], columns), jnp.float32)
    for row_tap in range(3):
        for col_tap in range(3):
            window = padded[:, 2 - row_tap:2 - row_tap + tile_rows, :, 2 - col_tap:2 - col_tap + columns]
            total = total + jnp.einsum('frow,co->frcw', window, kernel[:, 3 * row_tap + col_tap, :].astype(jnp.float32))
    return total

def kernel_grad(mixed, grad_sum):
    tile_rows = mixed.shape[1]
    columns = mixed.shape[3]
    padded = jnp.pad(mixed.astype(jnp.float32), ((0, 0), (1, 1), (0, 0), (1, 1)))
    grads = grad_sum.astype(jnp.float32)
    pieces = []
    for row_tap in range(3):
        for col_tap in range(3):
            window = padded[:, row_tap:row_tap + tile_rows, :, col_tap:col_tap + columns]
            pieces.append(jnp.einsum('frcw,frow->co', window, grads))
    return jnp.stack(pieces, axis=1)

def section(inputs, depth_taps, kernel):
    inputs32 = inputs.astype(jnp.float32)
    mixed = temporal(inputs32, depth_taps.astype(jnp.float32)).astype(jnp.bfloat16)
    summed = convolve(mixed, kernel)
    output = (inputs32 + jax.nn.silu(summed)).astype(jnp.bfloat16)
    return (mixed, summed, output)

def reference(features, taps, kern, proj):
    signal = features[0]
    cotangent = features[1].astype(jnp.float32) * (1.0 / math.sqrt(FRAMES * ROWS * WIDTH))
    mixed_a, summed_a, output_a = section(signal, taps[0], kern[0])
    latent = jnp.einsum('frcw,cl->frlw', output_a.astype(jnp.float32), proj[0].astype(jnp.float32)).astype(jnp.bfloat16)
    lifted = jnp.einsum('frlw,cl->frcw', latent.astype(jnp.float32), proj[1].astype(jnp.float32)).astype(jnp.bfloat16)
    mixed_b, summed_b, output_b = section(lifted, taps[1], kern[1])
    grad_b = (cotangent * squash(summed_b)).astype(jnp.bfloat16)
    back = adjoint(grad_b, kern[1])
    later_taps = taps[1].astype(jnp.float32)
    spread_back = later_taps[0][None, None, :, None] * back + later_taps[1][None, None, :, None] * advanced(back, 1) + later_taps[2][None, None, :, None] * advanced(back, 2)
    grad_in = (cotangent + spread_back).astype(jnp.bfloat16)
    grad_latent = jnp.einsum('frcw,cl->frlw', grad_in.astype(jnp.float32), proj[1].astype(jnp.float32)).astype(jnp.bfloat16)
    grad_out_a = jnp.einsum('frlw,cl->frcw', grad_latent.astype(jnp.float32), proj[0].astype(jnp.float32))
    grad_a = (grad_out_a * squash(summed_a)).astype(jnp.bfloat16)
    kernel_a = kernel_grad(mixed_a, grad_a)
    kernel_b = kernel_grad(mixed_b, grad_b)
    return (jnp.stack([output_a, output_b]), jnp.stack([kernel_a, kernel_b]))
```

```python
import functools
import math

import jax
import jax.numpy as jnp
from jax import lax
from jax.experimental import pallas as pl
from jax.experimental.pallas import tpu as pltpu
from jax.sharding import PartitionSpec as P

F32 = jnp.float32
BF16 = jnp.bfloat16
VMEM = pl.BlockSpec(memory_space=pltpu.VMEM)
SMEM = pl.BlockSpec(memory_space=pltpu.SMEM)
PARAMS = pltpu.CompilerParams(vmem_limit_bytes=40 * 1024 * 1024)


def dot(a, b):
    return lax.dot_general(a, b, (((1,), (0,)), ((), ())), preferred_element_type=F32)


def dot_nt(a, b):
    return lax.dot_general(a, b, (((1,), (1,)), ((), ())), preferred_element_type=F32)


def shifted(values, step):
    if step == 0:
        return values
    columns = values.shape[-1]
    lane = lax.broadcasted_iota(jnp.int32, values.shape, values.ndim - 1)
    edge = columns - 1 if step == 1 else 0
    moved = pltpu.roll(values, columns - 1 if step == 1 else 1, values.ndim - 1)
    return jnp.where(lane == edge, 0.0, moved)


def logistic(summed):
    return 1.0 / (1.0 + jnp.exp(-summed))


def tap_blocks(rows, outs):
    sums = []
    for row in range(len(rows) - 2):
        total = None
        for col_tap in range(3):
            part = None
            for row_tap in range(3):
                at = (3 * row_tap + col_tap) * outs
                block = rows[row + row_tap][at : at + outs]
                part = block if part is None else part + block
            part = shifted(part, col_tap - 1)
            total = part if total is None else total + part
        sums.append(total)
    return sums


def mix_kernel(tile, low, high, depth, extra, sent, own):
    frames, rows = tile.shape[0], tile.shape[1]
    peers = sent.shape[0]

    def row_of(frame, row):
        if row == 0:
            return low[frame, 0].astype(F32)
        if row == rows + 1:
            return high[frame, 0].astype(F32)
        return tile[frame, row - 1].astype(F32)

    weights = [depth[:, lag : lag + 1] for lag in range(3)]
    for row in range(rows + 2):
        history = [row_of(frame, row) for frame in range(frames)]
        for frame in range(frames):
            total = weights[0] * history[frame]
            for lag in range(1, 3):
                if frame >= lag:
                    total = total + weights[lag] * history[frame - lag]
            own[frame, row] = total.astype(BF16)
    for frame in range(frames):
        for row in range(rows + 2):
            block = own[frame, row]
            for peer in range(peers):
                sent[peer, frame * (rows + 2) + row] = block
    for peer in range(peers):
        sent[peer, frames * (rows + 2)] = extra[...]


def encode_kernel(place, gathered, taps_out, tile, proj_back, out, slope, sent, combo, combo_t):
    frames, rows, outs, columns = tile.shape
    peers, _, part, _ = gathered.shape
    channels = peers * part
    latents = proj_back.shape[0]

    @pl.when(place[0] == 0)
    def _():
        weights = taps_out[...]
        for frame in range(frames):
            products = []
            for row in range(0, rows + 2, 2):
                at = frame * (rows + 2) + row
                pair = jnp.concatenate(
                    [gathered[:, at + k].reshape(channels, columns) for k in range(2)], axis=1
                )
                both = dot(weights, pair)
                products += [both[:, :columns], both[:, columns:]]
            for row, summed in enumerate(tap_blocks(products, outs)):
                sigma = logistic(summed)
                result = (tile[frame, row].astype(F32) + summed * sigma).astype(BF16)
                out[frame, row] = result
                slope[frame, row] = sigma * (1.0 + summed * (1.0 - sigma))
                latent = dot(proj_back[...], result).astype(BF16)
                for peer in range(sent.shape[0]):
                    sent[peer, frame, row] = latent

    @pl.when(place[0] == 1)
    def _():
        factors = gathered[:, frames * (rows + 2)].reshape(channels, columns)
        merged = dot(taps_out[...], factors)
        combo[...] = merged.astype(BF16)
        combo_t[...] = merged.T.astype(BF16)
        sent[...] = jnp.zeros_like(sent)


def stacked(z_rows, frame, frames):
    blank = jnp.zeros_like(z_rows[0])
    return jnp.concatenate(
        [z_rows[frame - lag] if frame >= lag else blank for lag in range(3)], axis=0
    )


def z_row(low, mid, high, frame, row):
    rows = mid.shape[1]
    if row < rows:
        return low[frame, row]
    if row < 2 * rows:
        return mid[frame, row - rows]
    return high[frame, row - 2 * rows]


def decode_kernel(
    scale, place, low, mid, high, own, combo, combo_t, proj_out, proj_back, encoded, out, grad, sent
):
    frames, rows, latents, columns = mid.shape
    outs = own.shape[2]
    deep = 3 * latents

    @pl.when(place[0] == 0)
    def _():
        out[...] = encoded[...]
        sent[...] = jnp.zeros_like(sent)

    @pl.when(place[0] == 1)
    def _():
        weights = combo[...][:, :deep]
        back = combo_t[...][:deep]
        reach = 3 * rows
        mixed = []
        for frame in range(frames):
            wide = jnp.concatenate(
                [
                    stacked(
                        [z_row(low, mid, high, f, row) for f in range(frames)], frame, frames
                    )
                    for row in range(reach)
                ],
                axis=1,
            )
            both = dot(weights, wide)
            products = [both[:, row * columns : (row + 1) * columns] for row in range(reach)]
            moved = []
            for row, summed in enumerate(tap_blocks(products, outs)):
                sigma = logistic(summed)
                slope = sigma * (1.0 + summed * (1.0 - sigma))
                cotangent = own[frame, row].astype(F32) * scale
                slanted = (cotangent * slope).astype(BF16)
                moved.append(
                    [shifted(slanted.astype(F32), 1 - b).astype(BF16) for b in range(3)]
                )
                if 1 <= row <= rows:
                    lifted = dot(proj_out[...], mid[frame, row - 1]).astype(BF16)
                    out[frame, row - 1] = (lifted.astype(F32) + summed * sigma).astype(BF16)
                    grad[frame, row - 1] = slanted
            columns_of = [
                jnp.concatenate(
                    [moved[row - a + 2][b] for a in range(3) for b in range(3)], axis=0
                )
                for row in range(rows)
            ]
            mixed.append(dot(back, jnp.concatenate(columns_of, axis=1)))
        for frame in range(frames):
            total = mixed[frame][:latents]
            for lag in range(1, 3):
                if frame + lag < frames:
                    total = total + mixed[frame + lag][lag * latents : (lag + 1) * latents]
            for row in range(rows):
                direct = dot(proj_back[...], own[frame, row + 1]) * scale
                latent = (direct + total[:, row * columns : (row + 1) * columns]).astype(BF16)
                for peer in range(sent.shape[0]):
                    sent[peer, frame, row] = latent


def grad_kernel(
    place, arrived, slope, gathered, grad, low, mid, high, proj_out, send, keep, scratch
):
    frames, rows, outs, columns = slope.shape
    peers, _, part, _ = gathered.shape
    channels = peers * part
    latents = mid.shape[2]
    pairs, _, share, _ = scratch.shape
    halves = arrived.shape[0] // peers

    def window(grads, frame, row):
        blank = jnp.zeros((outs, columns), BF16)
        return jnp.concatenate(
            [
                grads[frame][row - a][b] if 0 <= row - a < rows else blank
                for a in range(3)
                for b in range(3)
            ],
            axis=0,
        )

    def steps(value):
        return [shifted(value.astype(F32), 1 - b).astype(BF16) for b in range(3)]

    def store(total):
        for pair in range(pairs):
            for side in range(2):
                at = (2 * pair + side) * share
                scratch[pair, side] = total[at : at + share]

    @pl.when(place[0] == 0)
    def _():
        grads = []
        for frame in range(frames):
            grads.append([])
            for row in range(rows):
                latent = arrived[1, frame, row].astype(F32)
                for peer in range(1, peers):
                    latent = latent + arrived[halves * peer + 1, frame, row].astype(F32)
                value = dot(proj_out[...], latent.astype(BF16)) * slope[frame, row]
                grads[-1].append(steps(value.astype(BF16)))
        spots = [(frame, row) for frame in range(frames) for row in range(rows + 2)]
        left = jnp.concatenate(
            [
                gathered[:, frame * (rows + 2) + row].reshape(channels, columns)
                for frame, row in spots
            ],
            axis=1,
        )
        right = jnp.concatenate([window(grads, frame, row) for frame, row in spots], axis=1)
        store(dot_nt(left, right))

    @pl.when(place[0] == 1)
    def _():
        grads = [[steps(grad[frame, row]) for row in range(rows)] for frame in range(frames)]
        spots = [(frame, row) for frame in range(frames) for row in range(rows + 2)]
        left = jnp.concatenate(
            [
                stacked(
                    [z_row(low, mid, high, f, row + 1) for f in range(frames)], frame, frames
                )
                for frame, row in spots
            ],
            axis=1,
        )
        right = jnp.concatenate([window(grads, frame, row) for frame, row in spots], axis=1)
        inner = dot_nt(left, right).astype(BF16)
        factors = gathered[:, frames * (rows + 2)].reshape(channels, columns)
        store(dot(factors[:, : 3 * latents], inner))

    mine = place[1]
    keep[...] = scratch[:, mine]
    send[...] = scratch[:, 1 - mine].astype(BF16)


def call(kernel, shapes, specs, scratch=()):
    return pl.pallas_call(
        kernel,
        out_shape=shapes,
        in_specs=specs,
        out_specs=jax.tree.map(lambda _: VMEM, shapes),
        scratch_shapes=list(scratch),
        compiler_params=PARAMS,
    )


def both_ways(low_side, high_side, axis):
    count = lax.axis_size(axis)
    forward = [(i, i + 1) for i in range(count - 1)]
    backward = [(i + 1, i) for i in range(count - 1)]
    return lax.ppermute(high_side, axis, forward), lax.ppermute(low_side, axis, backward)


def on_device(features, taps, kern, proj):
    shape = jax.ShapeDtypeStruct
    pipe = lax.axis_index("pipe")
    slab = lax.axis_index("slab")
    peers = lax.axis_size("chan")
    slabs = lax.axis_size("slab")
    both = peers * lax.axis_size("pipe")
    tile = features[0]
    frames, rows, part, columns = tile.shape
    channels, latents = proj.shape[1], proj.shape[2]
    share = channels // slabs
    offset = lax.axis_index("chan") * part
    place = jnp.stack([pipe, slab % 2]).astype(jnp.int32)
    scale = 1.0 / math.sqrt(frames * rows * slabs * columns)

    above, below = both_ways(tile[:, :1], tile[:, rows - 1 :], "slab")
    proj_out = lax.dynamic_slice_in_dim(proj[0], offset, part, 0)
    proj_back = proj_out.T
    depth = taps[0].astype(F32).T
    factors = (depth[:, :, None] * proj_out.astype(F32)[:, None, :]).reshape(part, 3 * latents)
    extra = jnp.pad(factors.astype(BF16), ((0, 0), (0, columns - 3 * latents)))
    depth = jnp.where(pipe == 0, depth, jnp.array([[1.0, 0.0, 0.0]], F32))
    sent, own = call(
        mix_kernel,
        (
            shape((peers, frames * (rows + 2) + 1, part, columns), BF16),
            shape((frames, rows + 2, part, columns), BF16),
        ),
        [VMEM] * 5,
    )(tile, above, below, depth, extra)
    gathered = lax.all_to_all(sent, "chan", 0, 0)

    out_cols = lax.dynamic_slice_in_dim(kern[0], offset, part, 2)
    taps_out = out_cols.transpose(1, 2, 0).reshape(9 * part, channels)
    tile_shape = (frames, rows, part, columns)
    latent_shape = (both, frames, rows, latents, columns)
    encoded, slope, sent, combo, combo_t = call(
        encode_kernel,
        (
            shape(tile_shape, BF16),
            shape(tile_shape, F32),
            shape(latent_shape, BF16),
            shape((9 * part, columns), BF16),
            shape((columns, 9 * part), BF16),
        ),
        [SMEM] + [VMEM] * 4,
    )(place, gathered, taps_out, tile, proj_back)

    arrived = lax.all_to_all(sent, ("chan", "pipe"), 0, 0)
    arrived = arrived.reshape((peers, 2) + latent_shape[1:])
    mid = jnp.sum(arrived[:, 0].astype(F32), axis=0).astype(BF16)
    low, high = both_ways(mid, mid, "slab")
    out, grad, sent = call(
        functools.partial(decode_kernel, scale),
        (shape(tile_shape, BF16), shape(tile_shape, BF16), shape(latent_shape, BF16)),
        [SMEM] + [VMEM] * 9,
    )(place, low, mid, high, own, combo, combo_t, proj_out, proj_back, encoded)

    arrived = lax.all_to_all(sent, ("chan", "pipe"), 0, 0)
    pairs = slabs // 2
    send, keep = call(
        grad_kernel,
        (shape((pairs, share, 9 * part), BF16), shape((pairs, share, 9 * part), F32)),
        [SMEM] + [VMEM] * 8,
        [pltpu.VMEM((pairs, 2, share, 9 * part), F32)],
    )(place, arrived, slope, gathered, grad, low, mid, high, proj_out)
    got = lax.ppermute(send, "slab", [(i, i ^ 1) for i in range(slabs)])
    halved = (keep + got.astype(F32)).astype(BF16)
    groups = [[2 * p + q for p in range(pairs)] for q in range(2)]
    pieces = lax.all_to_all(halved, "slab", 0, 0, axis_index_groups=groups)
    total = jnp.sum(pieces.astype(F32), axis=0).reshape(share, 9, part)
    return out[None], total[None]


def solution(mesh):
    placed = (
        P("pipe", None, "slab", "chan", None),
        P("pipe", None, "chan"),
        P("pipe", None, None, None),
        P("pipe", None, None),
    )
    return jax.shard_map(
        on_device,
        mesh=mesh,
        in_specs=placed,
        out_specs=(P("pipe", None, "slab", "chan", None), P("pipe", "slab", None, "chan")),
        check_vma=False,
    )
```

```python
import functools
import math

import jax
import jax.numpy as jnp
from jax import lax
from jax.experimental import pallas as pl
from jax.experimental.pallas import tpu as pltpu
from jax.sharding import PartitionSpec as P

F32 = jnp.float32
BF16 = jnp.bfloat16
VMEM = pl.BlockSpec(memory_space=pltpu.VMEM)
SMEM = pl.BlockSpec(memory_space=pltpu.SMEM)
PARAMS = pltpu.CompilerParams(vmem_limit_bytes=40 * 1024 * 1024)


def dot(a, b):
    return lax.dot_general(a, b, (((1,), (0,)), ((), ())), preferred_element_type=F32)


def dot_nt(a, b):
    return lax.dot_general(a, b, (((1,), (1,)), ((), ())), preferred_element_type=F32)


def shifted(values, step):
    if step == 0:
        return values
    columns = values.shape[-1]
    lane = lax.broadcasted_iota(jnp.int32, values.shape, values.ndim - 1)
    edge = columns - 1 if step == 1 else 0
    moved = pltpu.roll(values, columns - 1 if step == 1 else 1, values.ndim - 1)
    return jnp.where(lane == edge, 0.0, moved)


def logistic(summed):
    return 1.0 / (1.0 + jnp.exp(-summed))


def tap_blocks(rows, outs):
    sums = []
    for row in range(len(rows) - 2):
        total = None
        for col_tap in range(3):
            part = None
            for row_tap in range(3):
                at = (3 * row_tap + col_tap) * outs
                block = rows[row + row_tap][at : at + outs]
                part = block if part is None else part + block
            part = shifted(part, col_tap - 1)
            total = part if total is None else total + part
        sums.append(total)
    return sums


def block_of(gathered, at, part):
    rows = pl.ds(pl.multiple_of(at * part, part), part)
    return gathered[:, rows].reshape(gathered.shape[0] * part, gathered.shape[2])


def mix_kernel(tile, low, high, depth, extra, proj_back, sent, own):
    frames, rows, part, _ = tile.shape
    peers, latents = sent.shape[0], proj_back.shape[0]
    splits = peers // (frames * rows)

    def row_of(frame, row):
        if row == 0:
            return low[frame, 0].astype(F32)
        if row == rows + 1:
            return high[frame, 0].astype(F32)
        return tile[frame, row - 1].astype(F32)

    weights = [depth[:, lag : lag + 1] for lag in range(3)]
    for row in range(rows + 2):
        history = [row_of(frame, row) for frame in range(frames)]
        for frame in range(frames):
            total = weights[0] * history[frame]
            for lag in range(1, 3):
                if frame >= lag:
                    total = total + weights[lag] * history[frame - lag]
            block = total.astype(BF16)
            own[frame, row] = block
            at = (frame * (rows + 2) + row) * part
            for peer in range(peers):
                sent[peer, at : at + part] = block
    at = frames * (rows + 2) * part
    for peer in range(peers):
        sent[peer, at : at + part] = extra[...]
        row, turn = peer // splits, peer % splits
        if row < frames * rows and turn == 0:
            direct = dot(proj_back[...], tile[row // rows, row % rows]).astype(BF16)
        else:
            direct = jnp.zeros((latents, tile.shape[3]), BF16)
        sent[peer, at + part : at + part + latents] = direct


def encode_kernel(
    place, gathered, taps_out, tile, proj_t, kern, out, slope, sent, combo, wide_t, wide, held, done
):
    frames, rows, outs, columns = tile.shape
    peers = gathered.shape[0]
    part = outs
    channels = peers * part
    latents = proj_t.shape[0]
    deep = 3 * latents
    span = held.shape[2]
    splits = channels // span
    row_at, turn = place[1] // splits, place[1] % splits
    active = row_at < frames * rows
    fetch = pltpu.make_async_copy(
        kern.at[:, :, pl.ds(pl.multiple_of(turn * span, span), span)], held, done
    )
    fetch.start()

    @pl.when(place[0] == 0)
    def _():
        weights = taps_out[...]
        for frame in range(frames):
            products = []
            for row in range(0, rows + 2, 2):
                at = frame * (rows + 2) + row
                pair = jnp.concatenate(
                    [block_of(gathered, at + k, part) for k in range(2)], axis=1
                )
                both = dot(weights, pair)
                products += [both[:, :columns], both[:, columns:]]
            for row, summed in enumerate(tap_blocks(products, outs)):
                sigma = logistic(summed)
                out[frame, row] = (tile[frame, row].astype(F32) + summed * sigma).astype(BF16)
                slope[frame, row] = sigma * (1.0 + summed * (1.0 - sigma))

    fetch.wait()

    @pl.when(jnp.logical_and(place[0] == 0, active))
    def _():
        base = (row_at // rows) * (rows + 2) + row_at % rows
        turned = [block_of(gathered, base + a, part).T for a in range(3)]
        summed = None
        for b in range(3):
            total = None
            for a in range(3):
                term = dot(turned[a], held[3 * a + b])
                total = term if total is None else total + term
            if b != 1:
                line = lax.broadcasted_iota(jnp.int32, total.shape, 0)
                edge = columns - 1 if b == 2 else 0
                moved = pltpu.roll(total, columns - 1 if b == 2 else 1, 0)
                total = jnp.where(line == edge, 0.0, moved)
            summed = total if summed is None else summed + total
        bent = (summed * logistic(summed)).astype(BF16)
        latent = dot_nt(pick(proj_t, turn, span), bent)
        at = (frames * (rows + 2) + 1) * part
        for peer in range(peers):
            latent = latent + gathered[peer, at : at + latents].astype(F32)
        latent = latent.astype(BF16)
        for peer in range(sent.shape[0]):
            sent[peer] = latent

    @pl.when(jnp.logical_or(place[0] == 1, jnp.logical_not(active)))
    def _():
        sent[...] = jnp.zeros_like(sent)

    @pl.when(place[0] == 1)
    def _():
        factors = block_of(gathered, frames * (rows + 2), part)
        combo[...] = dot(taps_out[...], factors).astype(BF16)
        factors_t = factors.astype(F32).T.astype(BF16)[:deep]
        for tap in range(9):
            wide_t[tap * deep : (tap + 1) * deep] = dot(factors_t, held[tap]).astype(BF16)
        wide[...] = wide_t[...].astype(F32).T.astype(BF16)


def pick(ref, turn, span):
    chosen = ref[:, :span]
    for at in range(1, ref.shape[1] // span):
        chosen = jnp.where(turn == at, ref[:, at * span : (at + 1) * span], chosen)
    return chosen


def stacked(z_rows, frame, frames):
    blank = jnp.zeros_like(z_rows[0])
    return jnp.concatenate(
        [z_rows[frame - lag] if frame >= lag else blank for lag in range(3)], axis=0
    )


def z_row(low, mid, high, frame, row):
    rows = mid.shape[1]
    if row < rows:
        return low[frame, row]
    if row < 2 * rows:
        return mid[frame, row - rows]
    return high[frame, row - 2 * rows]


def decode_kernel(
    scale, place, low, mid, high, own, combo, wide_t, wide, gathered, proj_out, proj_t, encoded,
    out, grad, sent, bank
):
    frames, rows, latents, columns = mid.shape
    outs = own.shape[2]
    part = outs
    deep = 3 * latents
    span = wide.shape[0]
    peers = gathered.shape[0]
    splits = peers * part // span
    row_at, turn = place[1] // splits, place[1] % splits
    active = row_at < frames * rows

    @pl.when(place[0] == 0)
    def _():
        out[...] = encoded[...]

    @pl.when(jnp.logical_or(place[0] == 0, jnp.logical_not(active)))
    def _():
        sent[...] = jnp.zeros_like(sent)

    @pl.when(place[0] == 1)
    def _():
        weights = combo[...][:, :deep]
        reach = range(1, 3 * rows - 1)
        for frame in range(frames):
            band = jnp.concatenate(
                [
                    stacked(
                        [z_row(low, mid, high, f, row) for f in range(frames)], frame, frames
                    )
                    for row in reach
                ],
                axis=1,
            )
            both = dot(weights, band)
            products = [both[:, i * columns : (i + 1) * columns] for i in range(len(reach))]
            for row, summed in enumerate(tap_blocks(products, outs)):
                sigma = logistic(summed)
                cotangent = own[frame, row + 1].astype(F32) * scale
                slope = sigma * (1.0 + summed * (1.0 - sigma))
                grad[frame, row] = (cotangent * slope).astype(BF16)
                lifted = dot(proj_out[...], mid[frame, row]).astype(BF16)
                out[frame, row] = (lifted.astype(F32) + summed * sigma).astype(BF16)

    @pl.when(jnp.logical_and(place[0] == 1, active))
    def _():
        bank[:, 0:2] = jnp.zeros((3, 2) + bank.shape[2:], BF16)
        for frame in range(frames):
            for row in range(3 * rows):
                value = z_row(low, mid, high, frame, row).astype(F32)
                for b in range(3):
                    bank[b, frame + 2, row] = shifted(value, b - 1).astype(BF16)
        frame_at, line = row_at // rows, row_at % rows
        first = turn * (span // part)

        def channel_rows(frame, row):
            at = pl.multiple_of((frame * (rows + 2) + row) * part, part)
            block = gathered[pl.ds(first, span // part), pl.ds(at, part)]
            return block.reshape(span, columns)

        columns_of = []
        for lag in range(3):
            source = jnp.minimum(frame_at + lag, frames - 1)
            for a in range(3):
                columns_of.append(
                    jnp.concatenate(
                        [
                            bank[tap % 3, source - back + 2, line - a + 2 + tap // 3]
                            for tap in range(9)
                            for back in range(3)
                        ],
                        axis=0,
                    )
                )
        summed = dot(wide[...], jnp.concatenate(columns_of, axis=1))
        slanted, weights = [], []
        for lag in range(3):
            source = jnp.minimum(frame_at + lag, frames - 1)
            factor = jnp.where(frame_at + lag < frames, scale, 0.0)
            for a in range(3):
                at = (3 * lag + a) * columns
                value = summed[:, at : at + columns]
                sigma = logistic(value)
                slope = sigma * (1.0 + value * (1.0 - sigma))
                cotangent = channel_rows(source, line - a + 2).astype(F32) * factor
                slanted.append((cotangent * slope).astype(BF16))
                weights.append(
                    jnp.concatenate(
                        [
                            wide_t[(3 * a + b) * deep + lag * latents :][:latents]
                            for b in range(3)
                        ],
                        axis=0,
                    )
                )
        mixed = dot(jnp.concatenate(weights, axis=1), jnp.concatenate(slanted, axis=0))
        latent = dot(pick(proj_t, turn, span), channel_rows(frame_at, line + 1)) * scale
        for b in range(3):
            latent = latent + shifted(mixed[b * latents : (b + 1) * latents], 1 - b)
        latent = latent.astype(BF16)
        for peer in range(sent.shape[0]):
            sent[peer] = latent


def grad_kernel(place, arrived, slope, gathered, grad, low, mid, high, proj_out, sent):
    frames, rows, outs, columns = slope.shape
    peers = gathered.shape[0]
    part = outs
    latents = mid.shape[2]
    near, far, share, _ = sent.shape
    splits = peers // (frames * rows)

    def window(grads, frame, row):
        blank = jnp.zeros((outs, columns), BF16)
        return jnp.concatenate(
            [
                grads[frame][row - a][b] if 0 <= row - a < rows else blank
                for a in range(3)
                for b in range(3)
            ],
            axis=0,
        )

    def steps(value):
        return [shifted(value.astype(F32), 1 - b).astype(BF16) for b in range(3)]

    def store(total):
        for i in range(far):
            for j in range(near):
                at = (near * i + j) * share
                sent[j, i] = total[at : at + share].astype(BF16)

    spots = [(frame, row) for frame in range(frames) for row in range(rows + 2)]

    @pl.when(place[0] == 0)
    def _():
        grads = []
        for frame in range(frames):
            grads.append([])
            for row in range(rows):
                at = (frame * rows + row) * splits
                latent = arrived[2 * at + 1].astype(F32)
                for turn in range(1, splits):
                    latent = latent + arrived[2 * (at + turn) + 1].astype(F32)
                value = dot(proj_out[...], latent.astype(BF16)) * slope[frame, row]
                grads[-1].append(steps(value.astype(BF16)))
        left = jnp.concatenate(
            [block_of(gathered, at, part) for at in range(len(spots))], axis=1
        )
        right = jnp.concatenate([window(grads, frame, row) for frame, row in spots], axis=1)
        store(dot_nt(left, right))

    @pl.when(place[0] == 1)
    def _():
        grads = [[steps(grad[frame, row]) for row in range(rows)] for frame in range(frames)]
        left = jnp.concatenate(
            [
                stacked(
                    [z_row(low, mid, high, f, row + 1) for f in range(frames)], frame, frames
                )
                for frame, row in spots
            ],
            axis=1,
        )
        right = jnp.concatenate([window(grads, frame, row) for frame, row in spots], axis=1)
        inner = dot_nt(left, right).astype(BF16)
        factors = block_of(gathered, len(spots), part)
        store(dot(factors[:, : 3 * latents], inner))


def call(kernel, shapes, specs, scratch=()):
    return pl.pallas_call(
        kernel,
        out_shape=shapes,
        in_specs=specs,
        out_specs=jax.tree.map(lambda _: VMEM, shapes),
        scratch_shapes=list(scratch),
        compiler_params=PARAMS,
    )


def both_ways(low_side, high_side, axis):
    count = lax.axis_size(axis)
    forward = [(i, i + 1) for i in range(count - 1)]
    backward = [(i + 1, i) for i in range(count - 1)]
    return lax.ppermute(high_side, axis, forward), lax.ppermute(low_side, axis, backward)


def on_device(features, taps, kern, proj):
    shape = jax.ShapeDtypeStruct
    pipe = lax.axis_index("pipe")
    slab = lax.axis_index("slab")
    peers = lax.axis_size("chan")
    slabs = lax.axis_size("slab")
    both = peers * lax.axis_size("pipe")
    tile = features[0]
    frames, rows, part, columns = tile.shape
    channels, latents = proj.shape[1], proj.shape[2]
    share = channels // slabs
    offset = lax.axis_index("chan") * part
    place = jnp.stack([pipe, lax.axis_index("chan")]).astype(jnp.int32)
    scale = 1.0 / math.sqrt(frames * rows * slabs * columns)
    splits = peers // (frames * rows)
    span = channels // splits

    above, below = both_ways(tile[:, :1], tile[:, rows - 1 :], "slab")
    proj_t = proj[0].T
    proj_out = lax.dynamic_slice_in_dim(proj[0], offset, part, 0)
    proj_back = proj_out.T
    depth = taps[0].astype(F32).T
    factors = (depth[:, :, None] * proj_out.astype(F32)[:, None, :]).reshape(part, 3 * latents)
    extra = jnp.pad(factors.astype(BF16), ((0, 0), (0, columns - 3 * latents)))
    depth = jnp.where(pipe == 0, depth, jnp.array([[1.0, 0.0, 0.0]], F32))
    height = (frames * (rows + 2) + 1) * part + latents
    sent, own = call(
        mix_kernel,
        (
            shape((peers, height, columns), BF16),
            shape((frames, rows + 2, part, columns), BF16),
        ),
        [VMEM] * 6,
    )(tile, above, below, depth, extra, proj_back)
    gathered = lax.all_to_all(sent, "chan", 0, 0)

    out_cols = lax.dynamic_slice_in_dim(kern[0], offset, part, 2)
    taps_out = out_cols.transpose(1, 2, 0).reshape(9 * part, channels)
    tile_shape = (frames, rows, part, columns)
    latent_shape = (both, latents, columns)
    terms = 27 * latents
    encoded, slope, sent, combo, wide_t, wide = call(
        encode_kernel,
        (
            shape(tile_shape, BF16),
            shape(tile_shape, F32),
            shape(latent_shape, BF16),
            shape((9 * part, columns), BF16),
            shape((terms, span), BF16),
            shape((span, terms), BF16),
        ),
        [SMEM] + [VMEM] * 4 + [pl.BlockSpec(memory_space=pl.ANY)],
        [pltpu.VMEM((9, channels, span), BF16), pltpu.SemaphoreType.DMA],
    )(place, gathered, taps_out, tile, proj_t, kern[0].transpose(1, 0, 2))

    arrived = lax.all_to_all(sent, ("chan", "pipe"), 0, 0)
    arrived = arrived.reshape(peers, 2, latents, columns)[: frames * rows * splits, 0]
    arrived = arrived.reshape(frames, rows, splits, latents, columns)
    mid = jnp.sum(arrived.astype(F32), axis=2).astype(BF16)
    low, high = both_ways(mid, mid, "slab")
    out, grad, sent = call(
        functools.partial(decode_kernel, scale),
        (shape(tile_shape, BF16), shape(tile_shape, BF16), shape(latent_shape, BF16)),
        [SMEM] + [VMEM] * 11,
        [pltpu.VMEM((3, frames + 2, 3 * rows, latents, columns), BF16)],
    )(
        place, low, mid, high, own, combo, wide_t, wide, gathered, proj_out, proj_t, encoded
    )

    arrived = lax.all_to_all(sent, ("chan", "pipe"), 0, 0)
    near = 4
    far = slabs // near
    sent = call(
        grad_kernel,
        shape((near, far, share, 9 * part), BF16),
        [SMEM] + [VMEM] * 8,
    )(place, arrived, slope, gathered, grad, low, mid, high, proj_out)
    groups = [[near * i + j for j in range(near)] for i in range(far)]
    pieces = lax.all_to_all(sent, "slab", 0, 0, axis_index_groups=groups)
    partial = jnp.sum(pieces.astype(F32), axis=0).astype(BF16)
    groups = [[near * i + j for i in range(far)] for j in range(near)]
    pieces = lax.all_to_all(partial, "slab", 0, 0, axis_index_groups=groups)
    total = jnp.sum(pieces.astype(F32), axis=0).reshape(share, 9, part)
    return out[None], total[None]


def solution(mesh):
    placed = (
        P("pipe", None, "slab", "chan", None),
        P("pipe", None, "chan"),
        P("pipe", None, None, None),
        P("pipe", None, None),
    )
    return jax.shard_map(
        on_device,
        mesh=mesh,
        in_specs=placed,
        out_specs=(P("pipe", None, "slab", "chan", None), P("pipe", "slab", None, "chan")),
        check_vma=False,
    )
```

```python
import functools
import math

import jax
import jax.numpy as jnp
from jax import lax
from jax.experimental import pallas as pl
from jax.experimental.pallas import tpu as pltpu
from jax.sharding import PartitionSpec as P

F32 = jnp.float32
BF16 = jnp.bfloat16
VMEM = pl.BlockSpec(memory_space=pltpu.VMEM)
PARAMS = pltpu.CompilerParams(vmem_limit_bytes=40 * 1024 * 1024)


def dot(a, b):
    return lax.dot_general(a, b, (((1,), (0,)), ((), ())), preferred_element_type=F32)


def dot_nt(a, b):
    return lax.dot_general(a, b, (((1,), (1,)), ((), ())), preferred_element_type=F32)


def shifted(values, step):
    if step == 0:
        return values
    columns = values.shape[-1]
    lane = lax.broadcasted_iota(jnp.int32, values.shape, values.ndim - 1)
    edge = columns - 1 if step == 1 else 0
    moved = pltpu.roll(values, columns - 1 if step == 1 else 1, values.ndim - 1)
    return jnp.where(lane == edge, 0.0, moved)


def logistic(summed):
    return 1.0 / (1.0 + jnp.exp(-summed))


def tap_blocks(rows, outs):
    sums = []
    for row in range(len(rows) - 2):
        total = None
        for col_tap in range(3):
            part = None
            for row_tap in range(3):
                at = (3 * row_tap + col_tap) * outs
                block = rows[row + row_tap][at : at + outs]
                part = block if part is None else part + block
            part = shifted(part, col_tap - 1)
            total = part if total is None else total + part
        sums.append(total)
    return sums


def block_of(gathered, at, part):
    rows = pl.ds(pl.multiple_of(at * part, part), part)
    return gathered[:, rows].reshape(gathered.shape[0] * part, gathered.shape[2])


def column(row):
    count = row.shape[1]
    square = jnp.broadcast_to(row, (count, count))
    line = lax.broadcasted_iota(jnp.int32, square.shape, 0)
    lane = lax.broadcasted_iota(jnp.int32, square.shape, 1)
    return jnp.sum(jnp.where(line == lane, square, 0.0), axis=1, keepdims=True)


def mix_kernel(tile, low, high, taps, proj_t, sent, own, proj_out):
    frames, rows, part, columns = tile.shape
    peers, latents = sent.shape[0], proj_t.shape[0]
    splits = peers // (frames * rows)
    encoder = lax.axis_index("pipe") == 0

    def row_of(frame, row):
        if row == 0:
            return low[frame, rows - 1].astype(F32)
        if row == rows + 1:
            return high[frame, 0].astype(F32)
        return tile[frame, row - 1].astype(F32)

    proj_back = pick(proj_t, lax.axis_index("chan"), part)
    line = lax.broadcasted_iota(jnp.int32, (part, part), 0)
    lane = lax.broadcasted_iota(jnp.int32, (part, part), 1)
    turned = dot_nt(jnp.where(line == lane, 1.0, 0.0).astype(BF16), proj_back).astype(BF16)
    proj_out[...] = turned
    depth = [column(taps[lag : lag + 1].astype(F32)) for lag in range(3)]
    line = lax.broadcasted_iota(jnp.int32, (latents, columns), 0)
    lane = lax.broadcasted_iota(jnp.int32, (latents, columns), 1)
    extra = None
    for lag in range(3):
        spot = jnp.where(lane == line + lag * latents, 1.0, 0.0).astype(BF16)
        term = depth[lag] * dot(turned, spot)
        extra = term if extra is None else extra + term
    extra = extra.astype(BF16)
    weights = [
        jnp.where(encoder, depth[lag], 1.0 if lag == 0 else 0.0) for lag in range(3)
    ]
    for row in range(rows + 2):
        history = [row_of(frame, row) for frame in range(frames)]
        for frame in range(frames):
            total = weights[0] * history[frame]
            for lag in range(1, 3):
                if frame >= lag:
                    total = total + weights[lag] * history[frame - lag]
            block = total.astype(BF16)
            own[frame, row] = block
            at = (frame * (rows + 2) + row) * part
            for peer in range(peers):
                sent[peer, at : at + part] = block
    at = frames * (rows + 2) * part
    for peer in range(peers):
        sent[peer, at : at + part] = extra
        row, turn = peer // splits, peer % splits
        if row < frames * rows and turn == 0:
            direct = dot(proj_back, tile[row // rows, row % rows]).astype(BF16)
        else:
            direct = jnp.zeros((latents, columns), BF16)
        sent[peer, at + part : at + part + latents] = direct


def encode_kernel(
    gathered, taps_out, tile, proj_t, held, out, slope, sent, combo, wide_t, wide
):
    frames, rows, outs, columns = tile.shape
    peers = gathered.shape[0]
    part = outs
    channels = peers * part
    latents = proj_t.shape[0]
    deep = 3 * latents
    span = held.shape[2]
    splits = channels // span
    encoder, chan = lax.axis_index("pipe") == 0, lax.axis_index("chan")
    row_at, turn = chan // splits, chan % splits
    active = row_at < frames * rows

    @pl.when(encoder)
    def _():
        weights = taps_out[...]
        for frame in range(frames):
            products = []
            for row in range(0, rows + 2, 2):
                at = frame * (rows + 2) + row
                pair = jnp.concatenate(
                    [block_of(gathered, at + k, part) for k in range(2)], axis=1
                )
                both = dot(weights, pair)
                products += [both[:, :columns], both[:, columns:]]
            for row, summed in enumerate(tap_blocks(products, outs)):
                sigma = logistic(summed)
                out[frame, row] = (tile[frame, row].astype(F32) + summed * sigma).astype(BF16)
                slope[frame, row] = sigma * (1.0 + summed * (1.0 - sigma))

    @pl.when(jnp.logical_and(encoder, active))
    def _():
        base = (row_at // rows) * (rows + 2) + row_at % rows
        turned = [block_of(gathered, base + a, part).T for a in range(3)]
        summed = None
        for b in range(3):
            total = None
            for a in range(3):
                term = dot(turned[a], held[3 * a + b])
                total = term if total is None else total + term
            if b != 1:
                line = lax.broadcasted_iota(jnp.int32, total.shape, 0)
                edge = columns - 1 if b == 2 else 0
                moved = pltpu.roll(total, columns - 1 if b == 2 else 1, 0)
                total = jnp.where(line == edge, 0.0, moved)
            summed = total if summed is None else summed + total
        bent = (summed * logistic(summed)).astype(BF16)
        latent = dot_nt(pick(proj_t, turn, span), bent)
        at = (frames * (rows + 2) + 1) * part
        for peer in range(peers):
            latent = latent + gathered[peer, at : at + latents].astype(F32)
        latent = latent.astype(BF16)
        for peer in range(sent.shape[0]):
            sent[peer] = latent

    @pl.when(jnp.logical_not(jnp.logical_and(encoder, active)))
    def _():
        sent[...] = jnp.zeros_like(sent)

    @pl.when(jnp.logical_not(encoder))
    def _():
        factors = block_of(gathered, frames * (rows + 2), part)
        combo[...] = dot(taps_out[...], factors).astype(BF16)
        factors_t = factors.astype(F32).T.astype(BF16)[:deep]
        for tap in range(9):
            wide_t[tap * deep : (tap + 1) * deep] = dot(factors_t, held[tap]).astype(BF16)
        wide[...] = wide_t[...].astype(F32).T.astype(BF16)


def pick(ref, turn, span):
    chosen = ref[:, :span]
    for at in range(1, ref.shape[1] // span):
        chosen = jnp.where(turn == at, ref[:, at * span : (at + 1) * span], chosen)
    return chosen


def stacked(z_rows, frame, frames):
    blank = jnp.zeros_like(z_rows[0])
    return jnp.concatenate(
        [z_rows[frame - lag] if frame >= lag else blank for lag in range(3)], axis=0
    )


def z_row(low, mid, high, frame, row):
    rows = mid.shape[1]
    if row < rows:
        return low[frame, row]
    if row < 2 * rows:
        return mid[frame, row - rows]
    return high[frame, row - 2 * rows]


def decode_kernel(
    scale, low, mid, high, own, combo, wide_t, wide, gathered, proj_out, proj_t, encoded,
    out, grad, sent, bank
):
    frames, rows, latents, columns = mid.shape
    outs = own.shape[2]
    part = outs
    deep = 3 * latents
    span = wide.shape[0]
    peers = gathered.shape[0]
    splits = peers * part // span
    encoder, chan = lax.axis_index("pipe") == 0, lax.axis_index("chan")
    row_at, turn = chan // splits, chan % splits
    active = row_at < frames * rows

    @pl.when(encoder)
    def _():
        out[...] = encoded[...]

    @pl.when(jnp.logical_or(encoder, jnp.logical_not(active)))
    def _():
        sent[...] = jnp.zeros_like(sent)

    @pl.when(jnp.logical_not(encoder))
    def _():
        weights = combo[...][:, :deep]
        reach = range(1, 3 * rows - 1)
        for frame in range(frames):
            band = jnp.concatenate(
                [
                    stacked(
                        [z_row(low, mid, high, f, row) for f in range(frames)], frame, frames
                    )
                    for row in reach
                ],
                axis=1,
            )
            both = dot(weights, band)
            products = [both[:, i * columns : (i + 1) * columns] for i in range(len(reach))]
            for row, summed in enumerate(tap_blocks(products, outs)):
                sigma = logistic(summed)
                cotangent = own[frame, row + 1].astype(F32) * scale
                slope = sigma * (1.0 + summed * (1.0 - sigma))
                grad[frame, row] = (cotangent * slope).astype(BF16)
                lifted = dot(proj_out[...], mid[frame, row]).astype(BF16)
                out[frame, row] = (lifted.astype(F32) + summed * sigma).astype(BF16)

    @pl.when(jnp.logical_and(jnp.logical_not(encoder), active))
    def _():
        bank[:, 0:2] = jnp.zeros((3, 2) + bank.shape[2:], BF16)
        for frame in range(frames):
            for row in range(3 * rows):
                value = z_row(low, mid, high, frame, row).astype(F32)
                for b in range(3):
                    bank[b, frame + 2, row] = shifted(value, b - 1).astype(BF16)
        frame_at, line = row_at // rows, row_at % rows
        first = turn * (span // part)

        def channel_rows(frame, row):
            at = pl.multiple_of((frame * (rows + 2) + row) * part, part)
            block = gathered[pl.ds(first, span // part), pl.ds(at, part)]
            return block.reshape(span, columns)

        columns_of = []
        for lag in range(3):
            source = jnp.minimum(frame_at + lag, frames - 1)
            for a in range(3):
                columns_of.append(
                    jnp.concatenate(
                        [
                            bank[tap % 3, source - back + 2, line - a + 2 + tap // 3]
                            for tap in range(9)
                            for back in range(3)
                        ],
                        axis=0,
                    )
                )
        summed = dot(wide[...], jnp.concatenate(columns_of, axis=1))
        slanted, weights = [], []
        for lag in range(3):
            source = jnp.minimum(frame_at + lag, frames - 1)
            factor = jnp.where(frame_at + lag < frames, scale, 0.0)
            for a in range(3):
                at = (3 * lag + a) * columns
                value = summed[:, at : at + columns]
                sigma = logistic(value)
                slope = sigma * (1.0 + value * (1.0 - sigma))
                cotangent = channel_rows(source, line - a + 2).astype(F32) * factor
                slanted.append((cotangent * slope).astype(BF16))
                weights.append(
                    jnp.concatenate(
                        [
                            wide_t[(3 * a + b) * deep + lag * latents :][:latents]
                            for b in range(3)
                        ],
                        axis=0,
                    )
                )
        mixed = dot(jnp.concatenate(weights, axis=1), jnp.concatenate(slanted, axis=0))
        latent = dot(pick(proj_t, turn, span), channel_rows(frame_at, line + 1)) * scale
        for b in range(3):
            latent = latent + shifted(mixed[b * latents : (b + 1) * latents], 1 - b)
        latent = latent.astype(BF16)
        for peer in range(sent.shape[0]):
            sent[peer] = latent


def grad_kernel(
    arrived, slope, gathered, grad, low, mid, high, proj_out, send, keep, scratch
):
    frames, rows, outs, columns = slope.shape
    peers = gathered.shape[0]
    part = outs
    latents = mid.shape[2]
    pairs = scratch.shape[0]
    share = peers * part // (2 * pairs)
    encoder = lax.axis_index("pipe") == 0
    splits = peers // (frames * rows)

    def window(grads, frame, row):
        blank = jnp.zeros((outs, columns), BF16)
        return jnp.concatenate(
            [
                grads[frame][row - a][b] if 0 <= row - a < rows else blank
                for a in range(3)
                for b in range(3)
            ],
            axis=0,
        )

    def steps(value):
        return [shifted(value.astype(F32), 1 - b).astype(BF16) for b in range(3)]

    def store(total):
        wide = (9 * outs // columns) * columns
        for pair in range(pairs):
            for side in range(2):
                at = (2 * pair + side) * share
                block = total[at : at + share]
                for i in range(wide // columns):
                    scratch[pair, side, i * share : (i + 1) * share] = block[
                        :, i * columns : (i + 1) * columns
                    ]
                folds = columns // (9 * outs - wide)
                few = share // folds
                scratch[pair, side, wide // columns * share :] = jnp.concatenate(
                    [block[i * few : (i + 1) * few, wide:] for i in range(folds)], axis=1
                )

    spots = [(frame, row) for frame in range(frames) for row in range(rows + 2)]

    @pl.when(encoder)
    def _():
        grads = []
        for frame in range(frames):
            grads.append([])
            for row in range(rows):
                at = (frame * rows + row) * splits
                latent = arrived[2 * at + 1].astype(F32)
                for turn in range(1, splits):
                    latent = latent + arrived[2 * (at + turn) + 1].astype(F32)
                value = dot(proj_out[...], latent.astype(BF16)) * slope[frame, row]
                grads[-1].append(steps(value.astype(BF16)))
        left = jnp.concatenate(
            [block_of(gathered, at, part) for at in range(len(spots))], axis=1
        )
        right = jnp.concatenate([window(grads, frame, row) for frame, row in spots], axis=1)
        store(dot_nt(left, right))

    @pl.when(jnp.logical_not(encoder))
    def _():
        grads = [[steps(grad[frame, row]) for row in range(rows)] for frame in range(frames)]
        left = jnp.concatenate(
            [
                stacked(
                    [z_row(low, mid, high, f, row + 1) for f in range(frames)], frame, frames
                )
                for frame, row in spots
            ],
            axis=1,
        )
        right = jnp.concatenate([window(grads, frame, row) for frame, row in spots], axis=1)
        inner = dot_nt(left, right).astype(BF16)
        factors = block_of(gathered, len(spots), part)
        store(dot(factors[:, : 3 * latents], inner))

    mine = lax.axis_index("slab") % 2
    keep[...] = scratch[:, mine]
    send[...] = scratch[:, 1 - mine].astype(BF16)


def fold_kernel(pieces, out):
    taps, share, outs = out.shape
    columns = pieces.shape[2]
    total = pieces[0].astype(F32)
    for pair in range(1, pieces.shape[0]):
        total = total + pieces[pair].astype(F32)
    across = columns // outs
    for tap in range(taps - 1):
        at = tap // across * share
        lane = tap % across * outs
        out[tap] = total[at : at + share, lane : lane + outs]
    rest = total[(taps - 1) // across * share :]
    out[taps - 1] = jnp.concatenate(
        [rest[:, i * outs : (i + 1) * outs] for i in range(across)], axis=0
    )


def call(kernel, shapes, specs, scratch=()):
    return pl.pallas_call(
        kernel,
        out_shape=shapes,
        in_specs=specs,
        out_specs=jax.tree.map(lambda _: VMEM, shapes),
        scratch_shapes=list(scratch),
        compiler_params=PARAMS,
    )


def both_ways(low_side, high_side, axis):
    count = lax.axis_size(axis)
    forward = [(i, i + 1) for i in range(count - 1)]
    backward = [(i + 1, i) for i in range(count - 1)]
    return lax.ppermute(high_side, axis, forward), lax.ppermute(low_side, axis, backward)


def on_device(features, taps, kern, proj):
    shape = jax.ShapeDtypeStruct
    peers = lax.axis_size("chan")
    slabs = lax.axis_size("slab")
    both = peers * lax.axis_size("pipe")
    tile = features[0]
    frames, rows, part, columns = tile.shape
    channels, latents = proj.shape[1], proj.shape[2]
    share = channels // slabs
    chan = lax.axis_index("chan")
    offset = chan * part
    scale = 1.0 / math.sqrt(frames * rows * slabs * columns)
    splits = peers // (frames * rows)
    span = channels // splits

    above, below = both_ways(tile, tile, "slab")
    proj_t = proj[0].T
    height = (frames * (rows + 2) + 1) * part + latents
    sent, own, proj_out = call(
        mix_kernel,
        (
            shape((peers, height, columns), BF16),
            shape((frames, rows + 2, part, columns), BF16),
            shape((part, latents), BF16),
        ),
        [VMEM] * 5,
    )(tile, above, below, taps[0], proj_t)
    gathered = lax.all_to_all(sent, "chan", 0, 0)

    by_tap = kern[0].transpose(1, 0, 2)
    held = lax.dynamic_slice_in_dim(by_tap, chan % splits * span, span, 2)
    out_cols = lax.dynamic_slice_in_dim(kern[0], offset, part, 2)
    taps_out = out_cols.transpose(1, 2, 0).reshape(9 * part, channels)
    tile_shape = (frames, rows, part, columns)
    latent_shape = (both, latents, columns)
    terms = 27 * latents
    encoded, slope, sent, combo, wide_t, wide = call(
        encode_kernel,
        (
            shape(tile_shape, BF16),
            shape(tile_shape, F32),
            shape(latent_shape, BF16),
            shape((9 * part, columns), BF16),
            shape((terms, span), BF16),
            shape((span, terms), BF16),
        ),
        [VMEM] * 5,
    )(gathered, taps_out, tile, proj_t, held)

    arrived = lax.all_to_all(sent, ("chan", "pipe"), 0, 0)
    arrived = arrived.reshape(peers, 2, latents, columns)[: frames * rows * splits, 0]
    arrived = arrived.reshape(frames, rows, splits, latents, columns)
    mid = jnp.sum(arrived.astype(F32), axis=2).astype(BF16)
    low, high = both_ways(mid, mid, "slab")
    out, grad, sent = call(
        functools.partial(decode_kernel, scale),
        (shape(tile_shape, BF16), shape(tile_shape, BF16), shape(latent_shape, BF16)),
        [VMEM] * 11,
        [pltpu.VMEM((3, frames + 2, 3 * rows, latents, columns), BF16)],
    )(
        low, mid, high, own, combo, wide_t, wide, gathered, proj_out, proj_t, encoded
    )

    arrived = lax.all_to_all(sent, ("chan", "pipe"), 0, 0)
    pairs = slabs // 2
    lines = share * 9 * part // columns
    send, keep = call(
        grad_kernel,
        (shape((pairs, lines, columns), BF16), shape((pairs, lines, columns), F32)),
        [VMEM] * 8,
        [pltpu.VMEM((pairs, 2, lines, columns), F32)],
    )(arrived, slope, gathered, grad, low, mid, high, proj_out)
    got = lax.ppermute(send, "slab", [(i, i ^ 1) for i in range(slabs)])
    halved = (keep + got.astype(F32)).astype(BF16)
    groups = [[2 * p + q for p in range(pairs)] for q in range(2)]
    pieces = lax.all_to_all(halved, "slab", 0, 0, axis_index_groups=groups)
    total = call(fold_kernel, shape((9, share, part), F32), [VMEM])(pieces)
    total = total.transpose(1, 0, 2)
    return out[None], total[None]


def solution(mesh):
    placed = (
        P("pipe", None, "slab", "chan", None),
        P("pipe", None, "chan"),
        P("pipe", None, None, None),
        P("pipe", None, None),
    )
    return jax.shard_map(
        on_device,
        mesh=mesh,
        in_specs=placed,
        out_specs=(P("pipe", None, "slab", "chan", None), P("pipe", "slab", None, "chan")),
        check_vma=False,
    )
```

```python
import functools
import math

import jax
import jax.numpy as jnp
from jax import lax
from jax.experimental import pallas as pl
from jax.experimental.pallas import tpu as pltpu
from jax.sharding import PartitionSpec as P

F32 = jnp.float32
BF16 = jnp.bfloat16
VMEM = pl.BlockSpec(memory_space=pltpu.VMEM)
HBM = pl.BlockSpec(memory_space=pltpu.HBM)
PARAMS = pltpu.CompilerParams(vmem_limit_bytes=40 * 1024 * 1024)


def dot(a, b):
    return lax.dot_general(a, b, (((1,), (0,)), ((), ())), preferred_element_type=F32)


def dot_nt(a, b):
    return lax.dot_general(a, b, (((1,), (1,)), ((), ())), preferred_element_type=F32)


def shifted(values, step):
    if step == 0:
        return values
    columns = values.shape[-1]
    lane = lax.broadcasted_iota(jnp.int32, values.shape, values.ndim - 1)
    edge = columns - 1 if step == 1 else 0
    moved = pltpu.roll(values, columns - 1 if step == 1 else 1, values.ndim - 1)
    return jnp.where(lane == edge, 0.0, moved)


def logistic(summed):
    return 1.0 / (1.0 + jnp.exp(-summed))


def tap_blocks(rows, outs):
    sums = []
    for row in range(len(rows) - 2):
        total = None
        for col_tap in range(3):
            part = None
            for row_tap in range(3):
                at = (3 * row_tap + col_tap) * outs
                block = rows[row + row_tap][at : at + outs]
                part = block if part is None else part + block
            part = shifted(part, col_tap - 1)
            total = part if total is None else total + part
        sums.append(total)
    return sums


def block_of(pair, at, part, first=0, count=None):
    mine, theirs = pair
    count = mine.shape[0] if count is None else count
    rows = pl.ds(pl.multiple_of(at * part, part), part)
    left = mine[pl.ds(first, count), rows]
    right = theirs[pl.ds(first, count), rows]
    swap = lax.axis_index("chan") % 2 == 1
    even = jnp.where(swap, right, left)
    odd = jnp.where(swap, left, right)
    return jnp.concatenate([half[i] for i in range(count) for half in (even, odd)], axis=0)


def column(row):
    count = row.shape[1]
    square = jnp.broadcast_to(row, (count, count))
    line = lax.broadcasted_iota(jnp.int32, square.shape, 0)
    lane = lax.broadcasted_iota(jnp.int32, square.shape, 1)
    return jnp.sum(jnp.where(line == lane, square, 0.0), axis=1, keepdims=True)


def mix_weights(taps):
    encoder = lax.axis_index("pipe") == 0
    depth = [column(taps[lag : lag + 1].astype(F32)) for lag in range(3)]
    return [jnp.where(encoder, depth[lag], 1.0 if lag == 0 else 0.0) for lag in range(3)], depth


def mix_rows(history, weights):
    mixed = []
    for frame in range(len(history)):
        total = weights[0] * history[frame]
        for lag in range(1, 3):
            if frame >= lag:
                total = total + weights[lag] * history[frame - lag]
        mixed.append(total.astype(BF16))
    return mixed


def prepare_kernel(
    tile, taps, proj_t, kern, mid, extra, direct, proj_out, taps_out, held, done
):
    frames, rows, part, columns = tile.shape
    latents = proj_t.shape[0]
    chan = lax.axis_index("chan")
    across = columns // part
    lanes = pl.ds(pl.multiple_of(chan // across * columns, columns), columns)
    fetch = pltpu.make_async_copy(kern.at[:, :, lanes], held, done)
    fetch.start()
    proj_back = pick(proj_t, chan, part)
    line = lax.broadcasted_iota(jnp.int32, (part, part), 0)
    lane = lax.broadcasted_iota(jnp.int32, (part, part), 1)
    turned = dot_nt(jnp.where(line == lane, 1.0, 0.0).astype(BF16), proj_back).astype(BF16)
    proj_out[...] = turned
    weights, depth = mix_weights(taps)
    line = lax.broadcasted_iota(jnp.int32, (latents, columns), 0)
    lane = lax.broadcasted_iota(jnp.int32, (latents, columns), 1)
    total = None
    for lag in range(3):
        spot = jnp.where(lane == line + lag * latents, 1.0, 0.0).astype(BF16)
        term = depth[lag] * dot(turned, spot)
        total = term if total is None else total + term
    extra[...] = total.astype(BF16)
    for row in range(rows):
        mixed = mix_rows([tile[frame, row].astype(F32) for frame in range(frames)], weights)
        for frame in range(frames):
            mid[frame, row] = mixed[frame]
            direct[frame * rows + row] = dot(proj_back, tile[frame, row]).astype(BF16)
    fetch.wait()
    for tap in range(9):
        block = held[tap].T
        chosen = block[:part]
        for at in range(1, across):
            chosen = jnp.where(chan % across == at, block[at * part : (at + 1) * part], chosen)
        taps_out[tap * part : (tap + 1) * part] = chosen


def mix_kernel(low, high, taps, mid, extra, direct, sent, own):
    frames, rows, part, columns = mid.shape
    chips = sent.shape[0]
    latents = direct.shape[1]
    weights, _ = mix_weights(taps)
    before = mix_rows([low[frame, rows - 1].astype(F32) for frame in range(frames)], weights)
    after = mix_rows([high[frame, 0].astype(F32) for frame in range(frames)], weights)
    for frame in range(frames):
        blocks = [before[frame]] + [mid[frame, row] for row in range(rows)] + [after[frame]]
        for row in range(rows + 2):
            own[frame, row] = blocks[row]
            at = (frame * (rows + 2) + row) * part
            for chip in range(chips):
                sent[chip, at : at + part] = blocks[row]
    at = frames * (rows + 2) * part
    for chip in range(chips):
        sent[chip, at : at + part] = extra[...]
        if chip < frames * rows:
            sent[chip, at + part : at + part + latents] = direct[chip]
        else:
            sent[chip, at + part : at + part + latents] = jnp.zeros((latents, columns), BF16)


def encode_kernel(
    mine, theirs, taps_out, tile, proj_t, kern, out, slope, sent, combo, wide_t, wide, held, done
):
    frames, rows, outs, columns = tile.shape
    gathered = (mine, theirs)
    part = outs
    latents = proj_t.shape[0]
    deep = 3 * latents
    span = held.shape[2]
    encoder, chan = lax.axis_index("pipe") == 0, lax.axis_index("chan")
    row_at, turn = chan // 2, chan % 2
    fetch = pltpu.make_async_copy(
        kern.at[:, :, pl.ds(pl.multiple_of(turn * span, span), span)], held, done
    )
    fetch.start()
    active = row_at < frames * rows

    @pl.when(encoder)
    def _():
        weights = taps_out[...]
        for frame in range(frames):
            products = []
            for row in range(0, rows + 2, 2):
                at = frame * (rows + 2) + row
                pair = jnp.concatenate(
                    [block_of(gathered, at + k, part) for k in range(2)], axis=1
                )
                both = dot(weights, pair)
                products += [both[:, :columns], both[:, columns:]]
            for row, summed in enumerate(tap_blocks(products, outs)):
                sigma = logistic(summed)
                out[frame, row] = (tile[frame, row].astype(F32) + summed * sigma).astype(BF16)
                slope[frame, row] = sigma * (1.0 + summed * (1.0 - sigma))

    fetch.wait()

    @pl.when(jnp.logical_and(encoder, active))
    def _():
        base = (row_at // rows) * (rows + 2) + row_at % rows
        turned = [block_of(gathered, base + a, part).T for a in range(3)]
        summed = None
        for b in range(3):
            total = None
            for a in range(3):
                term = dot(turned[a], held[3 * a + b])
                total = term if total is None else total + term
            if b != 1:
                line = lax.broadcasted_iota(jnp.int32, total.shape, 0)
                edge = columns - 1 if b == 2 else 0
                moved = pltpu.roll(total, columns - 1 if b == 2 else 1, 0)
                total = jnp.where(line == edge, 0.0, moved)
            summed = total if summed is None else summed + total
        bent = (summed * logistic(summed)).astype(BF16)
        latent = dot_nt(pick(proj_t, turn, span), bent)
        at = (frames * (rows + 2) + 1) * part
        direct = jnp.zeros_like(latent)
        for chip in range(mine.shape[0]):
            for half in gathered:
                direct = direct + half[chip, at : at + latents].astype(F32)
        latent = (latent + jnp.where(turn == 0, direct, 0.0)).astype(BF16)
        for peer in range(sent.shape[0]):
            sent[peer] = latent

    @pl.when(jnp.logical_not(jnp.logical_and(encoder, active)))
    def _():
        sent[...] = jnp.zeros_like(sent)

    @pl.when(jnp.logical_not(encoder))
    def _():
        factors = block_of(gathered, frames * (rows + 2), part)
        combo[...] = dot(taps_out[...], factors).astype(BF16)
        factors_t = factors.astype(F32).T.astype(BF16)[:deep]
        for tap in range(9):
            wide_t[tap * deep : (tap + 1) * deep] = dot(factors_t, held[tap]).astype(BF16)
        wide[...] = wide_t[...].astype(F32).T.astype(BF16)


def pick(ref, turn, span):
    chosen = ref[:, :span]
    for at in range(1, ref.shape[1] // span):
        chosen = jnp.where(turn == at, ref[:, at * span : (at + 1) * span], chosen)
    return chosen


def stacked(z_rows, frame, frames):
    blank = jnp.zeros_like(z_rows[0])
    return jnp.concatenate(
        [z_rows[frame - lag] if frame >= lag else blank for lag in range(3)], axis=0
    )


def z_row(low, mid, high, frame, row):
    rows = mid.shape[1]
    if row < rows:
        return low[frame, row]
    if row < 2 * rows:
        return mid[frame, row - rows]
    return high[frame, row - 2 * rows]


def decode_kernel(
    scale, low, mid, high, own, combo, wide_t, wide, mine, theirs, proj_out, proj_t, encoded,
    out, grad, sent, bank
):
    frames, rows, latents, columns = mid.shape
    outs = own.shape[2]
    part = outs
    deep = 3 * latents
    span = wide.shape[0]
    gathered = (mine, theirs)
    encoder, chan = lax.axis_index("pipe") == 0, lax.axis_index("chan")
    row_at, turn = chan // 2, chan % 2
    active = row_at < frames * rows

    @pl.when(encoder)
    def _():
        out[...] = encoded[...]

    @pl.when(jnp.logical_or(encoder, jnp.logical_not(active)))
    def _():
        sent[...] = jnp.zeros_like(sent)

    @pl.when(jnp.logical_not(encoder))
    def _():
        weights = combo[...][:, :deep]
        reach = range(1, 3 * rows - 1)
        for frame in range(frames):
            band = jnp.concatenate(
                [
                    stacked(
                        [z_row(low, mid, high, f, row) for f in range(frames)], frame, frames
                    )
                    for row in reach
                ],
                axis=1,
            )
            both = dot(weights, band)
            products = [both[:, i * columns : (i + 1) * columns] for i in range(len(reach))]
            for row, summed in enumerate(tap_blocks(products, outs)):
                sigma = logistic(summed)
                cotangent = own[frame, row + 1].astype(F32) * scale
                slope = sigma * (1.0 + summed * (1.0 - sigma))
                grad[frame, row] = (cotangent * slope).astype(BF16)
                lifted = dot(proj_out[...], mid[frame, row]).astype(BF16)
                out[frame, row] = (lifted.astype(F32) + summed * sigma).astype(BF16)

    @pl.when(jnp.logical_and(jnp.logical_not(encoder), active))
    def _():
        bank[:, 0:2] = jnp.zeros((3, 2) + bank.shape[2:], BF16)
        for frame in range(frames):
            for row in range(3 * rows):
                value = z_row(low, mid, high, frame, row).astype(F32)
                for b in range(3):
                    bank[b, frame + 2, row] = shifted(value, b - 1).astype(BF16)
        frame_at, line = row_at // rows, row_at % rows
        chips = mine.shape[0] // 2

        def channel_rows(frame, row):
            return block_of(gathered, frame * (rows + 2) + row, part, turn * chips, chips)

        columns_of = []
        for lag in range(3):
            source = jnp.minimum(frame_at + lag, frames - 1)
            for a in range(3):
                columns_of.append(
                    jnp.concatenate(
                        [
                            bank[tap % 3, source - back + 2, line - a + 2 + tap // 3]
                            for tap in range(9)
                            for back in range(3)
                        ],
                        axis=0,
                    )
                )
        summed = dot(wide[...], jnp.concatenate(columns_of, axis=1))
        slanted, weights = [], []
        for lag in range(3):
            source = jnp.minimum(frame_at + lag, frames - 1)
            factor = jnp.where(frame_at + lag < frames, scale, 0.0)
            for a in range(3):
                at = (3 * lag + a) * columns
                value = summed[:, at : at + columns]
                sigma = logistic(value)
                slope = sigma * (1.0 + value * (1.0 - sigma))
                cotangent = channel_rows(source, line - a + 2).astype(F32) * factor
                slanted.append((cotangent * slope).astype(BF16))
                weights.append(
                    jnp.concatenate(
                        [
                            wide_t[(3 * a + b) * deep + lag * latents :][:latents]
                            for b in range(3)
                        ],
                        axis=0,
                    )
                )
        mixed = dot(jnp.concatenate(weights, axis=1), jnp.concatenate(slanted, axis=0))
        latent = dot(pick(proj_t, turn, span), channel_rows(frame_at, line + 1)) * scale
        for b in range(3):
            latent = latent + shifted(mixed[b * latents : (b + 1) * latents], 1 - b)
        latent = latent.astype(BF16)
        for peer in range(sent.shape[0]):
            sent[peer] = latent


def grad_kernel(
    arrived, slope, mine, theirs, grad, low, mid, high, proj_out, sent
):
    frames, rows, outs, columns = slope.shape
    gathered = (mine, theirs)
    part = outs
    near, far = sent.shape[:2]
    share = 2 * mine.shape[0] * part // (near * far)
    latents = mid.shape[2]
    encoder = lax.axis_index("pipe") == 0

    def window(grads, frame, row):
        blank = jnp.zeros((outs, columns), BF16)
        return jnp.concatenate(
            [
                grads[frame][row - a][b] if 0 <= row - a < rows else blank
                for a in range(3)
                for b in range(3)
            ],
            axis=0,
        )

    def steps(value):
        return [shifted(value.astype(F32), 1 - b).astype(BF16) for b in range(3)]

    def store(total):
        total = total.astype(BF16).astype(F32)
        wide = (9 * outs // columns) * columns
        folds = columns // (9 * outs - wide)
        few = share // folds
        for i in range(far):
            for j in range(near):
                at = (near * i + j) * share
                block = total[at : at + share]
                pieces = [block[:, k : k + columns] for k in range(0, wide, columns)]
                rest = [block[k * few : (k + 1) * few, wide:] for k in range(folds)]
                pieces.append(jnp.concatenate(rest, axis=1))
                sent[j, i] = jnp.concatenate(pieces, axis=0).astype(BF16)

    spots = [(frame, row) for frame in range(frames) for row in range(rows + 2)]

    @pl.when(encoder)
    def _():
        grads = []
        for frame in range(frames):
            grads.append([])
            for row in range(rows):
                at = 4 * (frame * rows + row)
                latent = arrived[at + 1].astype(F32) + arrived[at + 3].astype(F32)
                value = dot(proj_out[...], latent.astype(BF16)) * slope[frame, row]
                grads[-1].append(steps(value.astype(BF16)))
        left = jnp.concatenate(
            [block_of(gathered, at, part) for at in range(len(spots))], axis=1
        )
        right = jnp.concatenate([window(grads, frame, row) for frame, row in spots], axis=1)
        store(dot_nt(left, right))

    @pl.when(jnp.logical_not(encoder))
    def _():
        grads = [[steps(grad[frame, row]) for row in range(rows)] for frame in range(frames)]
        left = jnp.concatenate(
            [
                stacked(
                    [z_row(low, mid, high, f, row + 1) for f in range(frames)], frame, frames
                )
                for frame, row in spots
            ],
            axis=1,
        )
        right = jnp.concatenate([window(grads, frame, row) for frame, row in spots], axis=1)
        inner = dot_nt(left, right).astype(BF16)
        factors = block_of(gathered, len(spots), part)
        store(dot(factors[:, : 3 * latents], inner))


def fold_kernel(pieces, out):
    taps, share, outs = out.shape
    columns = pieces.shape[2]
    total = pieces[0].astype(F32)
    for pair in range(1, pieces.shape[0]):
        total = total + pieces[pair].astype(F32)
    across = columns // outs
    for tap in range(taps - 1):
        at = tap // across * share
        lane = tap % across * outs
        out[tap] = total[at : at + share, lane : lane + outs]
    rest = total[(taps - 1) // across * share :]
    out[taps - 1] = jnp.concatenate(
        [rest[:, i * outs : (i + 1) * outs] for i in range(across)], axis=0
    )


def call(kernel, shapes, specs, scratch=()):
    return pl.pallas_call(
        kernel,
        out_shape=shapes,
        in_specs=specs,
        out_specs=jax.tree.map(lambda _: VMEM, shapes),
        scratch_shapes=list(scratch),
        compiler_params=PARAMS,
    )


def both_ways(low_side, high_side, axis):
    count = lax.axis_size(axis)
    forward = [(i, i + 1) for i in range(count - 1)]
    backward = [(i + 1, i) for i in range(count - 1)]
    return lax.ppermute(high_side, axis, forward), lax.ppermute(low_side, axis, backward)


def on_device(features, taps, kern, proj):
    shape = jax.ShapeDtypeStruct
    peers = lax.axis_size("chan")
    slabs = lax.axis_size("slab")
    both = peers * lax.axis_size("pipe")
    tile = features[0]
    frames, rows, part, columns = tile.shape
    channels, latents = proj.shape[1], proj.shape[2]
    share = channels // slabs
    scale = 1.0 / math.sqrt(frames * rows * slabs * columns)
    span = channels // 2
    by_tap = kern[0].transpose(1, 0, 2)

    above, below = both_ways(tile, tile, "slab")
    proj_t = proj[0].T
    height = (frames * (rows + 2) + 1) * part + latents
    middle, extra, direct, proj_out, taps_out = call(
        prepare_kernel,
        (
            shape(tile.shape, BF16),
            shape((part, columns), BF16),
            shape((frames * rows, latents, columns), BF16),
            shape((part, latents), BF16),
            shape((9 * part, channels), BF16),
        ),
        [VMEM] * 3 + [HBM],
        [pltpu.VMEM((9, channels, columns), BF16), pltpu.SemaphoreType.DMA],
    )(tile, taps[0], proj_t, by_tap)
    sent, own = call(
        mix_kernel,
        (
            shape((peers // 2, height, columns), BF16),
            shape((frames, rows + 2, part, columns), BF16),
        ),
        [VMEM] * 6,
    )(above, below, taps[0], middle, extra, direct)
    groups = [[2 * chip + core for chip in range(peers // 2)] for core in range(2)]
    mine = lax.all_to_all(sent, "chan", 0, 0, axis_index_groups=groups)
    theirs = lax.ppermute(mine, "chan", [(i, i ^ 1) for i in range(peers)])

    tile_shape = (frames, rows, part, columns)
    latent_shape = (both, latents, columns)
    terms = 27 * latents
    encoded, slope, sent, combo, wide_t, wide = call(
        encode_kernel,
        (
            shape(tile_shape, BF16),
            shape(tile_shape, F32),
            shape(latent_shape, BF16),
            shape((9 * part, columns), BF16),
            shape((terms, span), BF16),
            shape((span, terms), BF16),
        ),
        [VMEM] * 5 + [HBM],
        [pltpu.VMEM((9, channels, span), BF16), pltpu.SemaphoreType.DMA],
    )(mine, theirs, taps_out, tile, proj_t, by_tap)

    arrived = lax.all_to_all(sent, ("chan", "pipe"), 0, 0)
    arrived = arrived.reshape(peers, 2, latents, columns)[: frames * rows * 2, 0]
    arrived = arrived.reshape(frames, rows, 2, latents, columns)
    mid = jnp.sum(arrived.astype(F32), axis=2).astype(BF16)
    low, high = both_ways(mid, mid, "slab")
    out, grad, sent = call(
        functools.partial(decode_kernel, scale),
        (shape(tile_shape, BF16), shape(tile_shape, BF16), shape(latent_shape, BF16)),
        [VMEM] * 12,
        [pltpu.VMEM((3, frames + 2, 3 * rows, latents, columns), BF16)],
    )(
        low, mid, high, own, combo, wide_t, wide, mine, theirs, proj_out, proj_t,
        encoded,
    )

    arrived = lax.all_to_all(sent, ("chan", "pipe"), 0, 0)
    near = 4
    far = slabs // near
    lines = share * 9 * part // columns
    sent = call(grad_kernel, shape((near, far, lines, columns), BF16), [VMEM] * 9)(
        arrived, slope, mine, theirs, grad, low, mid, high, proj_out
    )
    groups = [[near * i + j for j in range(near)] for i in range(far)]
    pieces = lax.all_to_all(sent, "slab", 0, 0, axis_index_groups=groups)
    partial = jnp.sum(pieces.astype(F32), axis=0).astype(BF16)
    groups = [[near * i + j for i in range(far)] for j in range(near)]
    pieces = lax.all_to_all(partial, "slab", 0, 0, axis_index_groups=groups)
    total = call(fold_kernel, shape((9, share, part), F32), [VMEM])(pieces)
    total = total.transpose(1, 0, 2)
    return out[None], total[None]


def solution(mesh):
    placed = (
        P("pipe", None, "slab", "chan", None),
        P("pipe", None, "chan"),
        P("pipe", None, None, None),
        P("pipe", None, None),
    )
    return jax.shard_map(
        on_device,
        mesh=mesh,
        in_specs=placed,
        out_specs=(P("pipe", None, "slab", "chan", None), P("pipe", "slab", None, "chan")),
        check_vma=False,
    )
```

```python
import functools
import math

import jax
import jax.numpy as jnp
from jax import lax
from jax.experimental import pallas as pl
from jax.experimental.pallas import tpu as pltpu
from jax.sharding import PartitionSpec as P

F32 = jnp.float32
BF16 = jnp.bfloat16
VMEM = pl.BlockSpec(memory_space=pltpu.VMEM)
HBM = pl.BlockSpec(memory_space=pltpu.HBM)


def dot(a, b):
    return lax.dot_general(a, b, (((1,), (0,)), ((), ())), preferred_element_type=F32)


def dot_nt(a, b):
    return lax.dot_general(a, b, (((1,), (1,)), ((), ())), preferred_element_type=F32)


def shifted(values, step):
    if step == 0:
        return values
    columns = values.shape[-1]
    lane = lax.broadcasted_iota(jnp.int32, values.shape, values.ndim - 1)
    edge = columns - 1 if step == 1 else 0
    moved = pltpu.roll(values, columns - 1 if step == 1 else 1, values.ndim - 1)
    return jnp.where(lane == edge, 0.0, moved)


def logistic(summed):
    return 1.0 / (1.0 + jnp.exp(-summed))


def tap_blocks(rows, outs):
    sums = []
    for row in range(len(rows) - 2):
        total = None
        for col_tap in range(3):
            part = None
            for row_tap in range(3):
                at = (3 * row_tap + col_tap) * outs
                block = rows[row + row_tap][at : at + outs]
                part = block if part is None else part + block
            part = shifted(part, col_tap - 1)
            total = part if total is None else total + part
        sums.append(total)
    return sums


def block_of(pair, at, part, first=0, count=None):
    mine, theirs = pair
    count = mine.shape[0] if count is None else count
    rows = pl.ds(pl.multiple_of(at * part, part), part)
    left = mine[pl.ds(first, count), rows]
    right = theirs[pl.ds(first, count), rows]
    swap = lax.axis_index("chan") % 2 == 1
    even = jnp.where(swap, right, left)
    odd = jnp.where(swap, left, right)
    return jnp.concatenate([half[i] for i in range(count) for half in (even, odd)], axis=0)


def column(row):
    count = row.shape[1]
    square = jnp.broadcast_to(row, (count, count))
    line = lax.broadcasted_iota(jnp.int32, square.shape, 0)
    lane = lax.broadcasted_iota(jnp.int32, square.shape, 1)
    return jnp.sum(jnp.where(line == lane, square, 0.0), axis=1, keepdims=True)


def mix_weights(taps):
    encoder = lax.axis_index("pipe") == 0
    depth = [column(taps[lag : lag + 1].astype(F32)) for lag in range(3)]
    return [jnp.where(encoder, depth[lag], 1.0 if lag == 0 else 0.0) for lag in range(3)], depth


def mix_rows(history, weights):
    mixed = []
    for frame in range(len(history)):
        total = weights[0] * history[frame]
        for lag in range(1, 3):
            if frame >= lag:
                total = total + weights[lag] * history[frame - lag]
        mixed.append(total.astype(BF16))
    return mixed


def prepare_kernel(
    tile, taps, proj_t, kern, mid, extra, direct, proj_out, taps_out, held, done
):
    frames, rows, part, columns = tile.shape
    latents = proj_t.shape[0]
    chan = lax.axis_index("chan")
    across = columns // part
    lanes = pl.ds(pl.multiple_of(chan // across * columns, columns), columns)
    fetch = pltpu.make_async_copy(kern.at[:, :, lanes], held, done)
    fetch.start()
    proj_back = pick(proj_t, chan, part)
    line = lax.broadcasted_iota(jnp.int32, (part, part), 0)
    lane = lax.broadcasted_iota(jnp.int32, (part, part), 1)
    turned = dot_nt(jnp.where(line == lane, 1.0, 0.0).astype(BF16), proj_back).astype(BF16)
    proj_out[...] = turned
    weights, depth = mix_weights(taps)
    line = lax.broadcasted_iota(jnp.int32, (latents, columns), 0)
    lane = lax.broadcasted_iota(jnp.int32, (latents, columns), 1)
    total = None
    for lag in range(3):
        spot = jnp.where(lane == line + lag * latents, 1.0, 0.0).astype(BF16)
        term = depth[lag] * dot(turned, spot)
        total = term if total is None else total + term
    extra[...] = total.astype(BF16)
    for row in range(rows):
        mixed = mix_rows([tile[frame, row].astype(F32) for frame in range(frames)], weights)
        for frame in range(frames):
            mid[frame, row] = mixed[frame]
            direct[frame * rows + row] = dot(proj_back, tile[frame, row]).astype(BF16)
    fetch.wait()
    for tap in range(9):
        block = held[tap].T
        chosen = block[:part]
        for at in range(1, across):
            chosen = jnp.where(chan % across == at, block[at * part : (at + 1) * part], chosen)
        taps_out[tap * part : (tap + 1) * part] = chosen


def mix_kernel(low, high, taps, mid, extra, direct, sent, own):
    frames, rows, part, columns = mid.shape
    chips = sent.shape[0]
    latents = direct.shape[1]
    weights, _ = mix_weights(taps)
    before = mix_rows([low[frame, rows - 1].astype(F32) for frame in range(frames)], weights)
    after = mix_rows([high[frame, 0].astype(F32) for frame in range(frames)], weights)
    for frame in range(frames):
        blocks = [before[frame]] + [mid[frame, row] for row in range(rows)] + [after[frame]]
        for row in range(rows + 2):
            own[frame, row] = blocks[row]
            at = (frame * (rows + 2) + row) * part
            for chip in range(chips):
                sent[chip, at : at + part] = blocks[row]
    at = frames * (rows + 2) * part
    for chip in range(chips):
        sent[chip, at : at + part] = extra[...]
        if chip < frames * rows:
            sent[chip, at + part : at + part + latents] = direct[chip]
        else:
            sent[chip, at + part : at + part + latents] = jnp.zeros((latents, columns), BF16)


def encode_kernel(
    mine, theirs, taps_out, tile, proj_t, kern, out, slope, sent, combo, wide_t, wide
):
    frames, rows, outs, columns = tile.shape
    gathered = (mine, theirs)
    part = outs
    latents = proj_t.shape[0]
    deep = 3 * latents
    span = wide.shape[0]
    encoder, chan = lax.axis_index("pipe") == 0, lax.axis_index("chan")
    row_at, turn = chan // 2, chan % 2
    active = row_at < frames * rows

    @pl.when(encoder)
    def _():
        weights = taps_out[...]
        for frame in range(frames):
            products = []
            for row in range(0, rows + 2, 2):
                at = frame * (rows + 2) + row
                pair = jnp.concatenate(
                    [block_of(gathered, at + k, part) for k in range(2)], axis=1
                )
                both = dot(weights, pair)
                products += [both[:, :columns], both[:, columns:]]
            for row, summed in enumerate(tap_blocks(products, outs)):
                sigma = logistic(summed)
                out[frame, row] = (tile[frame, row].astype(F32) + summed * sigma).astype(BF16)
                slope[frame, row] = sigma * (1.0 + summed * (1.0 - sigma))

    @pl.when(jnp.logical_and(encoder, active))
    def _():
        base = (row_at // rows) * (rows + 2) + row_at % rows
        turned = [block_of(gathered, base + a, part).T for a in range(3)]
        summed = None
        for b in range(3):
            total = None
            for a in range(3):
                term = dot(turned[a], kern[3 * a + b])
                total = term if total is None else total + term
            if b != 1:
                line = lax.broadcasted_iota(jnp.int32, total.shape, 0)
                edge = columns - 1 if b == 2 else 0
                moved = pltpu.roll(total, columns - 1 if b == 2 else 1, 0)
                total = jnp.where(line == edge, 0.0, moved)
            summed = total if summed is None else summed + total
        bent = (summed * logistic(summed)).astype(BF16)
        latent = dot_nt(proj_t[...], bent)
        at = (frames * (rows + 2) + 1) * part
        for chip in range(mine.shape[0]):
            for half in gathered:
                latent = latent + half[chip, at : at + latents].astype(F32)
        few = latents // 2
        latent = jnp.where(turn == 0, latent[:few], latent[few:]).astype(BF16)
        for peer in range(sent.shape[0]):
            sent[peer] = latent

    @pl.when(jnp.logical_not(jnp.logical_and(encoder, active)))
    def _():
        sent[...] = jnp.zeros_like(sent)

    @pl.when(jnp.logical_not(encoder))
    def _():
        factors = block_of(gathered, frames * (rows + 2), part)
        combo[...] = dot(taps_out[...], factors).astype(BF16)
        factors_t = factors.astype(F32).T.astype(BF16)[:deep]
        for tap in range(9):
            block = pick(kern.at[tap], turn, span)
            wide_t[tap * deep : (tap + 1) * deep] = dot(factors_t, block).astype(BF16)
        wide[...] = wide_t[...].astype(F32).T.astype(BF16)


def pick(ref, turn, span):
    chosen = ref[:, :span]
    for at in range(1, ref.shape[1] // span):
        chosen = jnp.where(turn == at, ref[:, at * span : (at + 1) * span], chosen)
    return chosen


def stacked(z_rows, frame, frames):
    blank = jnp.zeros_like(z_rows[0])
    return jnp.concatenate(
        [z_rows[frame - lag] if frame >= lag else blank for lag in range(3)], axis=0
    )


def z_row(low, mid, high, frame, row):
    rows = mid.shape[1]
    if row < rows:
        return low[frame, row]
    if row < 2 * rows:
        return mid[frame, row - rows]
    return high[frame, row - 2 * rows]


def decode_kernel(
    scale, low, mid, high, own, combo, wide_t, wide, mine, theirs, proj_out, proj_t, encoded,
    out, grad, sent, bank
):
    frames, rows, latents, columns = mid.shape
    outs = own.shape[2]
    part = outs
    deep = 3 * latents
    span = wide.shape[0]
    gathered = (mine, theirs)
    encoder, chan = lax.axis_index("pipe") == 0, lax.axis_index("chan")
    row_at, turn = chan // 2, chan % 2
    active = row_at < frames * rows

    @pl.when(encoder)
    def _():
        out[...] = encoded[...]

    @pl.when(jnp.logical_or(encoder, jnp.logical_not(active)))
    def _():
        sent[...] = jnp.zeros_like(sent)

    @pl.when(jnp.logical_not(encoder))
    def _():
        weights = combo[...][:, :deep]
        reach = range(1, 3 * rows - 1)
        for frame in range(frames):
            band = jnp.concatenate(
                [
                    stacked(
                        [z_row(low, mid, high, f, row) for f in range(frames)], frame, frames
                    )
                    for row in reach
                ],
                axis=1,
            )
            both = dot(weights, band)
            products = [both[:, i * columns : (i + 1) * columns] for i in range(len(reach))]
            for row, summed in enumerate(tap_blocks(products, outs)):
                sigma = logistic(summed)
                cotangent = own[frame, row + 1].astype(F32) * scale
                slope = sigma * (1.0 + summed * (1.0 - sigma))
                grad[frame, row] = (cotangent * slope).astype(BF16)
                lifted = dot(proj_out[...], mid[frame, row]).astype(BF16)
                out[frame, row] = (lifted.astype(F32) + summed * sigma).astype(BF16)

    @pl.when(jnp.logical_and(jnp.logical_not(encoder), active))
    def _():
        bank[:, 0:2] = jnp.zeros((3, 2) + bank.shape[2:], BF16)
        for frame in range(frames):
            for row in range(3 * rows):
                value = z_row(low, mid, high, frame, row).astype(F32)
                for b in range(3):
                    bank[b, frame + 2, row] = shifted(value, b - 1).astype(BF16)
        frame_at, line = row_at // rows, row_at % rows
        chips = mine.shape[0] // 2

        def channel_rows(frame, row):
            return block_of(gathered, frame * (rows + 2) + row, part, turn * chips, chips)

        columns_of = []
        for lag in range(3):
            source = jnp.minimum(frame_at + lag, frames - 1)
            for a in range(3):
                columns_of.append(
                    jnp.concatenate(
                        [
                            bank[tap % 3, source - back + 2, line - a + 2 + tap // 3]
                            for tap in range(9)
                            for back in range(3)
                        ],
                        axis=0,
                    )
                )
        summed = dot(wide[...], jnp.concatenate(columns_of, axis=1))
        slanted, weights = [], []
        for lag in range(3):
            source = jnp.minimum(frame_at + lag, frames - 1)
            factor = jnp.where(frame_at + lag < frames, scale, 0.0)
            for a in range(3):
                at = (3 * lag + a) * columns
                value = summed[:, at : at + columns]
                sigma = logistic(value)
                slope = sigma * (1.0 + value * (1.0 - sigma))
                cotangent = channel_rows(source, line - a + 2).astype(F32) * factor
                slanted.append((cotangent * slope).astype(BF16))
                weights.append(
                    jnp.concatenate(
                        [
                            wide_t[(3 * a + b) * deep + lag * latents :][:latents]
                            for b in range(3)
                        ],
                        axis=0,
                    )
                )
        mixed = dot(jnp.concatenate(weights, axis=1), jnp.concatenate(slanted, axis=0))
        latent = dot(pick(proj_t, turn, span), channel_rows(frame_at, line + 1)) * scale
        for b in range(3):
            latent = latent + shifted(mixed[b * latents : (b + 1) * latents], 1 - b)
        latent = latent.astype(BF16)
        for peer in range(sent.shape[0]):
            sent[peer] = latent


def grad_kernel(
    arrived, slope, mine, theirs, grad, low, mid, high, proj_out, sent
):
    frames, rows, outs, columns = slope.shape
    gathered = (mine, theirs)
    part = outs
    near, far = sent.shape[:2]
    share = 2 * mine.shape[0] * part // (near * far)
    latents = mid.shape[2]
    encoder = lax.axis_index("pipe") == 0

    def window(grads, frame, row):
        blank = jnp.zeros((outs, columns), BF16)
        return jnp.concatenate(
            [
                grads[frame][row - a][b] if 0 <= row - a < rows else blank
                for a in range(3)
                for b in range(3)
            ],
            axis=0,
        )

    def steps(value):
        return [shifted(value.astype(F32), 1 - b).astype(BF16) for b in range(3)]

    def store(total):
        total = total.astype(BF16).astype(F32)
        wide = (9 * outs // columns) * columns
        folds = columns // (9 * outs - wide)
        few = share // folds
        for i in range(far):
            for j in range(near):
                at = (near * i + j) * share
                block = total[at : at + share]
                pieces = [block[:, k : k + columns] for k in range(0, wide, columns)]
                rest = [block[k * few : (k + 1) * few, wide:] for k in range(folds)]
                pieces.append(jnp.concatenate(rest, axis=1))
                sent[j, i] = jnp.concatenate(pieces, axis=0).astype(BF16)

    spots = [(frame, row) for frame in range(frames) for row in range(rows + 2)]

    @pl.when(encoder)
    def _():
        grads = []
        for frame in range(frames):
            grads.append([])
            for row in range(rows):
                at = 4 * (frame * rows + row)
                latent = arrived[at + 1].astype(F32) + arrived[at + 3].astype(F32)
                value = dot(proj_out[...], latent.astype(BF16)) * slope[frame, row]
                grads[-1].append(steps(value.astype(BF16)))
        left = jnp.concatenate(
            [block_of(gathered, at, part) for at in range(len(spots))], axis=1
        )
        right = jnp.concatenate([window(grads, frame, row) for frame, row in spots], axis=1)
        store(dot_nt(left, right))

    @pl.when(jnp.logical_not(encoder))
    def _():
        grads = [[steps(grad[frame, row]) for row in range(rows)] for frame in range(frames)]
        left = jnp.concatenate(
            [
                stacked(
                    [z_row(low, mid, high, f, row + 1) for f in range(frames)], frame, frames
                )
                for frame, row in spots
            ],
            axis=1,
        )
        right = jnp.concatenate([window(grads, frame, row) for frame, row in spots], axis=1)
        inner = dot_nt(left, right).astype(BF16)
        factors = block_of(gathered, len(spots), part)
        store(dot(factors[:, : 3 * latents], inner))


def fold_kernel(pieces, out):
    taps, share, outs = out.shape
    columns = pieces.shape[2]
    total = pieces[0].astype(F32)
    for pair in range(1, pieces.shape[0]):
        total = total + pieces[pair].astype(F32)
    across = columns // outs
    for tap in range(taps - 1):
        at = tap // across * share
        lane = tap % across * outs
        out[tap] = total[at : at + share, lane : lane + outs]
    rest = total[(taps - 1) // across * share :]
    out[taps - 1] = jnp.concatenate(
        [rest[:, i * outs : (i + 1) * outs] for i in range(across)], axis=0
    )


def call(kernel, shapes, specs, scratch=(), limit=40):
    return pl.pallas_call(
        kernel,
        out_shape=shapes,
        in_specs=specs,
        out_specs=jax.tree.map(lambda _: VMEM, shapes),
        scratch_shapes=list(scratch),
        compiler_params=pltpu.CompilerParams(vmem_limit_bytes=limit * 1024 * 1024),
    )


def both_ways(low_side, high_side, axis):
    count = lax.axis_size(axis)
    forward = [(i, i + 1) for i in range(count - 1)]
    backward = [(i + 1, i) for i in range(count - 1)]
    return lax.ppermute(high_side, axis, forward), lax.ppermute(low_side, axis, backward)


def on_device(features, taps, kern, proj):
    shape = jax.ShapeDtypeStruct
    peers = lax.axis_size("chan")
    slabs = lax.axis_size("slab")
    both = peers * lax.axis_size("pipe")
    tile = features[0]
    frames, rows, part, columns = tile.shape
    channels, latents = proj.shape[1], proj.shape[2]
    share = channels // slabs
    scale = 1.0 / math.sqrt(frames * rows * slabs * columns)
    span = channels // 2
    by_tap = kern[0].transpose(1, 0, 2)

    above, below = both_ways(tile, tile, "slab")
    proj_t = proj[0].T
    height = (frames * (rows + 2) + 1) * part + latents
    middle, extra, direct, proj_out, taps_out = call(
        prepare_kernel,
        (
            shape(tile.shape, BF16),
            shape((part, columns), BF16),
            shape((frames * rows, latents, columns), BF16),
            shape((part, latents), BF16),
            shape((9 * part, channels), BF16),
        ),
        [VMEM] * 3 + [HBM],
        [pltpu.VMEM((9, channels, columns), BF16), pltpu.SemaphoreType.DMA],
        limit=52,
    )(tile, taps[0], proj_t, by_tap)
    sent, own = call(
        mix_kernel,
        (
            shape((peers // 2, height, columns), BF16),
            shape((frames, rows + 2, part, columns), BF16),
        ),
        [VMEM] * 6,
    )(above, below, taps[0], middle, extra, direct)
    groups = [[2 * chip + core for chip in range(peers // 2)] for core in range(2)]
    mine = lax.all_to_all(sent, "chan", 0, 0, axis_index_groups=groups)
    theirs = lax.ppermute(mine, "chan", [(i, i ^ 1) for i in range(peers)])

    tile_shape = (frames, rows, part, columns)
    latent_shape = (both, latents, columns)
    terms = 27 * latents
    encoded, slope, sent, combo, wide_t, wide = call(
        encode_kernel,
        (
            shape(tile_shape, BF16),
            shape(tile_shape, F32),
            shape((both, latents // 2, columns), BF16),
            shape((9 * part, columns), BF16),
            shape((terms, span), BF16),
            shape((span, terms), BF16),
        ),
        [VMEM] * 6,
    )(mine, theirs, taps_out, tile, proj_t, by_tap)

    arrived = lax.all_to_all(sent, ("chan", "pipe"), 0, 0)
    arrived = arrived.reshape(peers, 2, latents // 2, columns)[: frames * rows * 2, 0]
    mid = arrived.reshape(frames, rows, latents, columns)
    low, high = both_ways(mid, mid, "slab")
    out, grad, sent = call(
        functools.partial(decode_kernel, scale),
        (shape(tile_shape, BF16), shape(tile_shape, BF16), shape(latent_shape, BF16)),
        [VMEM] * 12,
        [pltpu.VMEM((3, frames + 2, 3 * rows, latents, columns), BF16)],
    )(
        low, mid, high, own, combo, wide_t, wide, mine, theirs, proj_out, proj_t,
        encoded,
    )

    arrived = lax.all_to_all(sent, ("chan", "pipe"), 0, 0)
    near = 4
    far = slabs // near
    lines = share * 9 * part // columns
    sent = call(grad_kernel, shape((near, far, lines, columns), BF16), [VMEM] * 9)(
        arrived, slope, mine, theirs, grad, low, mid, high, proj_out
    )
    groups = [[near * i + j for j in range(near)] for i in range(far)]
    pieces = lax.all_to_all(sent, "slab", 0, 0, axis_index_groups=groups)
    partial = jnp.sum(pieces.astype(F32), axis=0).astype(BF16)
    groups = [[near * i + j for i in range(far)] for j in range(near)]
    pieces = lax.all_to_all(partial, "slab", 0, 0, axis_index_groups=groups)
    total = call(fold_kernel, shape((9, share, part), F32), [VMEM])(pieces)
    total = total.transpose(1, 0, 2)
    return out[None], total[None]


def solution(mesh):
    placed = (
        P("pipe", None, "slab", "chan", None),
        P("pipe", None, "chan"),
        P("pipe", None, None, None),
        P("pipe", None, None),
    )
    return jax.shard_map(
        on_device,
        mesh=mesh,
        in_specs=placed,
        out_specs=(P("pipe", None, "slab", "chan", None), P("pipe", "slab", None, "chan")),
        check_vma=False,
    )
```

```python
import functools
import math

import jax
import jax.numpy as jnp
from jax import lax
from jax.experimental import pallas as pl
from jax.experimental.pallas import tpu as pltpu
from jax.sharding import PartitionSpec as P

F32 = jnp.float32
BF16 = jnp.bfloat16
VMEM = pl.BlockSpec(memory_space=pltpu.VMEM)
HBM = pl.BlockSpec(memory_space=pltpu.HBM)


def dot(a, b):
    return lax.dot_general(a, b, (((1,), (0,)), ((), ())), preferred_element_type=F32)


def dot_nt(a, b):
    return lax.dot_general(a, b, (((1,), (1,)), ((), ())), preferred_element_type=F32)


def shifted(values, step):
    if step == 0:
        return values
    columns = values.shape[-1]
    lane = lax.broadcasted_iota(jnp.int32, values.shape, values.ndim - 1)
    edge = columns - 1 if step == 1 else 0
    moved = pltpu.roll(values, columns - 1 if step == 1 else 1, values.ndim - 1)
    return jnp.where(lane == edge, 0.0, moved)


def logistic(summed):
    return 1.0 / (1.0 + jnp.exp(-summed))


def tap_blocks(rows, outs):
    sums = []
    for row in range(len(rows) - 2):
        total = None
        for col_tap in range(3):
            part = None
            for row_tap in range(3):
                at = (3 * row_tap + col_tap) * outs
                block = rows[row + row_tap][at : at + outs]
                part = block if part is None else part + block
            part = shifted(part, col_tap - 1)
            total = part if total is None else total + part
        sums.append(total)
    return sums


def block_of(pair, at, part):
    mine, theirs = pair
    count = mine.shape[0]
    rows = pl.ds(pl.multiple_of(at * part, part), part)
    left, right = mine[:, rows], theirs[:, rows]
    swap = lax.axis_index("chan") % 2 == 1
    even = jnp.where(swap, right, left)
    odd = jnp.where(swap, left, right)
    return jnp.concatenate([half[i] for i in range(count) for half in (even, odd)], axis=0)


def column(row):
    count = row.shape[1]
    square = jnp.broadcast_to(row, (count, count))
    line = lax.broadcasted_iota(jnp.int32, square.shape, 0)
    lane = lax.broadcasted_iota(jnp.int32, square.shape, 1)
    return jnp.sum(jnp.where(line == lane, square, 0.0), axis=1, keepdims=True)


def mix_weights(taps):
    encoder = lax.axis_index("pipe") == 0
    depth = [column(taps[lag : lag + 1].astype(F32)) for lag in range(3)]
    return [jnp.where(encoder, depth[lag], 1.0 if lag == 0 else 0.0) for lag in range(3)], depth


def mix_rows(history, weights):
    mixed = []
    for frame in range(len(history)):
        total = weights[0] * history[frame]
        for lag in range(1, 3):
            if frame >= lag:
                total = total + weights[lag] * history[frame - lag]
        mixed.append(total.astype(BF16))
    return mixed


def prepare_kernel(tile, taps, proj_t, mid, extra, direct, proj_out):
    frames, rows, part, columns = tile.shape
    latents = proj_t.shape[0]
    chan = lax.axis_index("chan")
    proj_back = pick(proj_t, chan, part)
    line = lax.broadcasted_iota(jnp.int32, (part, part), 0)
    lane = lax.broadcasted_iota(jnp.int32, (part, part), 1)
    turned = dot_nt(jnp.where(line == lane, 1.0, 0.0).astype(BF16), proj_back).astype(BF16)
    proj_out[...] = turned
    weights, depth = mix_weights(taps)
    line = lax.broadcasted_iota(jnp.int32, (latents, columns), 0)
    lane = lax.broadcasted_iota(jnp.int32, (latents, columns), 1)
    total = None
    for lag in range(3):
        spot = jnp.where(lane == line + lag * latents, 1.0, 0.0).astype(BF16)
        term = depth[lag] * dot(turned, spot)
        total = term if total is None else total + term
    extra[...] = total.astype(BF16)
    for row in range(rows):
        mixed = mix_rows([tile[frame, row].astype(F32) for frame in range(frames)], weights)
        for frame in range(frames):
            mid[frame, row] = mixed[frame]
            direct[frame * rows + row] = dot(proj_back, tile[frame, row]).astype(BF16)

def turn_kernel(after, kern, taps_out, held, done):
    columns = held.shape[2]
    part = taps_out.shape[0] // 9
    chan = lax.axis_index("chan")
    across = columns // part
    lanes = pl.ds(pl.multiple_of(chan // across * columns, columns), columns)
    fetch = pltpu.make_async_copy(kern.at[:, :, lanes], held, done)
    fetch.start()
    fetch.wait()
    for tap in range(9):
        block = held[tap].T
        chosen = block[:part]
        for at in range(1, across):
            chosen = jnp.where(chan % across == at, block[at * part : (at + 1) * part], chosen)
        taps_out[tap * part : (tap + 1) * part] = chosen


def mix_kernel(low, high, taps, mid, extra, direct, sent, own):
    frames, rows, part, columns = mid.shape
    chips = sent.shape[0]
    latents = direct.shape[1]
    weights, _ = mix_weights(taps)
    before = mix_rows([low[frame, rows - 1].astype(F32) for frame in range(frames)], weights)
    after = mix_rows([high[frame, 0].astype(F32) for frame in range(frames)], weights)
    for frame in range(frames):
        blocks = [before[frame]] + [mid[frame, row] for row in range(rows)] + [after[frame]]
        for row in range(rows + 2):
            own[frame, row] = blocks[row]
            at = (frame * (rows + 2) + row) * part
            for chip in range(chips):
                sent[chip, at : at + part] = blocks[row]
    at = frames * (rows + 2) * part
    encoder = lax.axis_index("pipe") == 0
    blank = jnp.zeros((part - latents, columns), BF16)
    for chip in range(chips):
        first = direct[min(chip, frames * rows - 1)]
        last = jnp.where(encoder, jnp.concatenate([first, blank], axis=0), extra[...])
        sent[chip, at : at + part] = last


def encode_kernel(
    mine, theirs, taps_out, proj_t, kern, sent, combo, wide_t, wide, *, frames, rows
):
    columns = mine.shape[2]
    gathered = (mine, theirs)
    part = taps_out.shape[0] // 9
    latents = proj_t.shape[0]
    deep = 3 * latents
    encoder, chan = lax.axis_index("pipe") == 0, lax.axis_index("chan")
    row_at, turn = chan // 2, chan % 2
    active = row_at < frames * rows

    @pl.when(jnp.logical_and(encoder, active))
    def _():
        base = (row_at // rows) * (rows + 2) + row_at % rows
        turned = [block_of(gathered, base + a, part).T for a in range(3)]
        summed = None
        for b in range(3):
            total = None
            for a in range(3):
                term = dot(turned[a], kern[3 * a + b])
                total = term if total is None else total + term
            if b != 1:
                line = lax.broadcasted_iota(jnp.int32, total.shape, 0)
                edge = columns - 1 if b == 2 else 0
                moved = pltpu.roll(total, columns - 1 if b == 2 else 1, 0)
                total = jnp.where(line == edge, 0.0, moved)
            summed = total if summed is None else summed + total
        bent = (summed * logistic(summed)).astype(BF16)
        latent = dot_nt(proj_t[...], bent)
        at = frames * (rows + 2) * part
        for chip in range(mine.shape[0]):
            for half in gathered:
                latent = latent + half[chip, at : at + latents].astype(F32)
        few = latents // 2
        latent = jnp.where(turn == 0, latent[:few], latent[few:]).astype(BF16)
        for peer in range(sent.shape[0]):
            sent[peer] = latent

    @pl.when(jnp.logical_not(jnp.logical_and(encoder, active)))
    def _():
        sent[...] = jnp.zeros_like(sent)

    @pl.when(jnp.logical_not(encoder))
    def _():
        factors = block_of(gathered, frames * (rows + 2), part)
        combo[...] = dot(taps_out[...], factors).astype(BF16)
        factors_t = factors.astype(F32).T.astype(BF16)[:deep]
        for tap in range(9):
            wide_t[tap * deep : (tap + 1) * deep] = dot(factors_t, kern[tap]).astype(BF16)
        wide[...] = wide_t[...].astype(F32).T.astype(BF16)


def pick(ref, turn, span):
    chosen = ref[:, :span]
    for at in range(1, ref.shape[1] // span):
        chosen = jnp.where(turn == at, ref[:, at * span : (at + 1) * span], chosen)
    return chosen


def stacked(z_rows, frame, frames):
    blank = jnp.zeros_like(z_rows[0])
    return jnp.concatenate(
        [z_rows[frame - lag] if frame >= lag else blank for lag in range(3)], axis=0
    )


def z_row(low, mid, high, frame, row):
    rows = mid.shape[1]
    if row < rows:
        return low[frame, row]
    if row < 2 * rows:
        return mid[frame, row - rows]
    return high[frame, row - 2 * rows]


def decode_kernel(
    scale, low, mid, high, own, combo, wide_t, wide, mine, theirs, proj_out, proj_t, taps_out, tile,
    out, slope, grad, sent, bank
):
    frames, rows, latents, columns = mid.shape
    outs = own.shape[2]
    part = outs
    deep = 3 * latents
    channels = wide.shape[0]
    gathered = (mine, theirs)
    encoder, chan = lax.axis_index("pipe") == 0, lax.axis_index("chan")
    row_at, turn = chan // 2, chan % 2
    active = row_at < frames * rows

    @pl.when(encoder)
    def _():
        weights = taps_out[...]
        for frame in range(frames):
            products = []
            for row in range(0, rows + 2, 2):
                at = frame * (rows + 2) + row
                pair = jnp.concatenate(
                    [block_of(gathered, at + k, part) for k in range(2)], axis=1
                )
                both = dot(weights, pair)
                products += [both[:, :columns], both[:, columns:]]
            for row, summed in enumerate(tap_blocks(products, outs)):
                sigma = logistic(summed)
                out[frame, row] = (tile[frame, row].astype(F32) + summed * sigma).astype(BF16)
                slope[frame, row] = sigma * (1.0 + summed * (1.0 - sigma))

    @pl.when(jnp.logical_or(encoder, jnp.logical_not(active)))
    def _():
        sent[...] = jnp.zeros_like(sent)

    @pl.when(jnp.logical_not(encoder))
    def _():
        weights = combo[...][:, :deep]
        reach = range(1, 3 * rows - 1)
        for frame in range(frames):
            band = jnp.concatenate(
                [
                    stacked(
                        [z_row(low, mid, high, f, row) for f in range(frames)], frame, frames
                    )
                    for row in reach
                ],
                axis=1,
            )
            both = dot(weights, band)
            products = [both[:, i * columns : (i + 1) * columns] for i in range(len(reach))]
            for row, summed in enumerate(tap_blocks(products, outs)):
                sigma = logistic(summed)
                cotangent = own[frame, row + 1].astype(F32) * scale
                bend = sigma * (1.0 + summed * (1.0 - sigma))
                grad[frame, row] = (cotangent * bend).astype(BF16)
                lifted = dot(proj_out[...], mid[frame, row]).astype(BF16)
                out[frame, row] = (lifted.astype(F32) + summed * sigma).astype(BF16)

    @pl.when(jnp.logical_and(jnp.logical_not(encoder), active))
    def _():
        bank[:, 0:2] = jnp.zeros((3, 2) + bank.shape[2:], BF16)
        for frame in range(frames):
            for row in range(3 * rows):
                value = z_row(low, mid, high, frame, row).astype(F32)
                for b in range(3):
                    bank[b, frame + 2, row] = shifted(value, b - 1).astype(BF16)
        frame_at, line = row_at // rows, row_at % rows
        def channel_rows(frame, row):
            return block_of(gathered, frame * (rows + 2) + row, part)

        columns_of = []
        for lag in range(3):
            source = jnp.minimum(frame_at + lag, frames - 1)
            for a in range(3):
                columns_of.append(
                    jnp.concatenate(
                        [
                            bank[tap % 3, source - back + 2, line - a + 2 + tap // 3]
                            for tap in range(9)
                            for back in range(3)
                        ],
                        axis=0,
                    )
                )
        summed = dot(wide[...], jnp.concatenate(columns_of, axis=1))
        slanted, weights = [], []
        for lag in range(3):
            source = jnp.minimum(frame_at + lag, frames - 1)
            factor = jnp.where(frame_at + lag < frames, scale, 0.0)
            for a in range(3):
                at = (3 * lag + a) * columns
                value = summed[:, at : at + columns]
                sigma = logistic(value)
                bend = sigma * (1.0 + value * (1.0 - sigma))
                cotangent = channel_rows(source, line - a + 2).astype(F32) * factor
                slanted.append((cotangent * bend).astype(BF16))
                weights.append(
                    jnp.concatenate(
                        [
                            wide_t[(3 * a + b) * deep + lag * latents :][:latents]
                            for b in range(3)
                        ],
                        axis=0,
                    )
                )
        mixed = dot(jnp.concatenate(weights, axis=1), jnp.concatenate(slanted, axis=0))
        latent = dot(proj_t[...], channel_rows(frame_at, line + 1)) * scale
        for b in range(3):
            latent = latent + shifted(mixed[b * latents : (b + 1) * latents], 1 - b)
        few = latents // 2
        latent = jnp.where(turn == 0, latent[:few], latent[few:]).astype(BF16)
        for peer in range(sent.shape[0]):
            sent[peer] = latent


def grad_kernel(
    arrived, slope, mine, theirs, grad, low, mid, high, proj_out, sent
):
    frames, rows, outs, columns = slope.shape
    gathered = (mine, theirs)
    part = outs
    near, far = sent.shape[:2]
    share = 2 * mine.shape[0] * part // (near * far)
    latents = mid.shape[2]
    encoder = lax.axis_index("pipe") == 0

    def window(grads, frame, row):
        blank = jnp.zeros((outs, columns), BF16)
        return jnp.concatenate(
            [
                grads[frame][row - a][b] if 0 <= row - a < rows else blank
                for a in range(3)
                for b in range(3)
            ],
            axis=0,
        )

    def steps(value):
        return [shifted(value.astype(F32), 1 - b).astype(BF16) for b in range(3)]

    def store(total):
        total = total.astype(BF16).astype(F32)
        wide = (9 * outs // columns) * columns
        folds = columns // (9 * outs - wide)
        few = share // folds
        for i in range(far):
            for j in range(near):
                at = (near * i + j) * share
                block = total[at : at + share]
                pieces = [block[:, k : k + columns] for k in range(0, wide, columns)]
                rest = [block[k * few : (k + 1) * few, wide:] for k in range(folds)]
                pieces.append(jnp.concatenate(rest, axis=1))
                sent[j, i] = jnp.concatenate(pieces, axis=0).astype(BF16)

    spots = [(frame, row) for frame in range(frames) for row in range(rows + 2)]

    @pl.when(encoder)
    def _():
        grads = []
        for frame in range(frames):
            grads.append([])
            for row in range(rows):
                at = 4 * (frame * rows + row)
                latent = jnp.concatenate(
                    [arrived[at + 1].astype(F32), arrived[at + 3].astype(F32)], axis=0
                )
                value = dot(proj_out[...], latent.astype(BF16)) * slope[frame, row]
                grads[-1].append(steps(value.astype(BF16)))
        left = jnp.concatenate(
            [block_of(gathered, at, part) for at in range(len(spots))], axis=1
        )
        right = jnp.concatenate([window(grads, frame, row) for frame, row in spots], axis=1)
        store(dot_nt(left, right))

    @pl.when(jnp.logical_not(encoder))
    def _():
        grads = [[steps(grad[frame, row]) for row in range(rows)] for frame in range(frames)]
        left = jnp.concatenate(
            [
                stacked(
                    [z_row(low, mid, high, f, row + 1) for f in range(frames)], frame, frames
                )
                for frame, row in spots
            ],
            axis=1,
        )
        right = jnp.concatenate([window(grads, frame, row) for frame, row in spots], axis=1)
        inner = dot_nt(left, right).astype(BF16)
        factors = block_of(gathered, len(spots), part)
        store(dot(factors[:, : 3 * latents], inner))


def fold_kernel(pieces, out):
    taps, share, outs = out.shape
    columns = pieces.shape[2]
    total = pieces[0].astype(F32)
    for pair in range(1, pieces.shape[0]):
        total = total + pieces[pair].astype(F32)
    across = columns // outs
    for tap in range(taps - 1):
        at = tap // across * share
        lane = tap % across * outs
        out[tap] = total[at : at + share, lane : lane + outs]
    rest = total[(taps - 1) // across * share :]
    out[taps - 1] = jnp.concatenate(
        [rest[:, i * outs : (i + 1) * outs] for i in range(across)], axis=0
    )


def call(kernel, shapes, specs, scratch=(), limit=40):
    return pl.pallas_call(
        kernel,
        out_shape=shapes,
        in_specs=specs,
        out_specs=jax.tree.map(lambda _: VMEM, shapes),
        scratch_shapes=list(scratch),
        compiler_params=pltpu.CompilerParams(vmem_limit_bytes=limit * 1024 * 1024),
    )


def both_ways(low_side, high_side, axis):
    count = lax.axis_size(axis)
    forward = [(i, i + 1) for i in range(count - 1)]
    backward = [(i + 1, i) for i in range(count - 1)]
    return lax.ppermute(high_side, axis, forward), lax.ppermute(low_side, axis, backward)


def on_device(features, taps, kern, proj):
    shape = jax.ShapeDtypeStruct
    peers = lax.axis_size("chan")
    slabs = lax.axis_size("slab")
    both = peers * lax.axis_size("pipe")
    tile = features[0]
    frames, rows, part, columns = tile.shape
    channels, latents = proj.shape[1], proj.shape[2]
    share = channels // slabs
    scale = 1.0 / math.sqrt(frames * rows * slabs * columns)
    by_tap = kern[0].transpose(1, 0, 2)

    above, below = both_ways(tile, tile, "slab")
    proj_t = proj[0].T
    height = (frames * (rows + 2) + 1) * part
    middle, extra, direct, proj_out = call(
        prepare_kernel,
        (
            shape(tile.shape, BF16),
            shape((part, columns), BF16),
            shape((frames * rows, latents, columns), BF16),
            shape((part, latents), BF16),
        ),
        [VMEM] * 3,
    )(tile, taps[0], proj_t)
    sent, own = call(
        mix_kernel,
        (
            shape((peers // 2, height, columns), BF16),
            shape((frames, rows + 2, part, columns), BF16),
        ),
        [VMEM] * 6,
    )(above, below, taps[0], middle, extra, direct)
    groups = [[2 * chip + core for chip in range(peers // 2)] for core in range(2)]
    mine = lax.all_to_all(sent, "chan", 0, 0, axis_index_groups=groups)
    theirs = lax.ppermute(mine, "chan", [(i, i ^ 1) for i in range(peers)])

    taps_out = call(
        turn_kernel,
        shape((9 * part, channels), BF16),
        [HBM] * 2,
        [pltpu.VMEM((9, channels, columns), BF16), pltpu.SemaphoreType.DMA],
        limit=51,
    )(mine, by_tap)
    tile_shape = (frames, rows, part, columns)
    latent_shape = (both, latents // 2, columns)
    terms = 27 * latents
    sent, combo, wide_t, wide = call(
        functools.partial(encode_kernel, frames=frames, rows=rows),
        (
            shape(latent_shape, BF16),
            shape((9 * part, columns), BF16),
            shape((terms, channels), BF16),
            shape((channels, terms), BF16),
        ),
        [VMEM] * 5,
    )(mine, theirs, taps_out, proj_t, by_tap)

    arrived = lax.all_to_all(sent, ("chan", "pipe"), 0, 0)
    arrived = arrived.reshape(peers, 2, latents // 2, columns)[: frames * rows * 2, 0]
    mid = arrived.reshape(frames, rows, latents, columns)
    low, high = both_ways(mid, mid, "slab")
    out, slope, grad, sent = call(
        functools.partial(decode_kernel, scale),
        (
            shape(tile_shape, BF16),
            shape(tile_shape, F32),
            shape(tile_shape, BF16),
            shape(latent_shape, BF16),
        ),
        [VMEM] * 13,
        [pltpu.VMEM((3, frames + 2, 3 * rows, latents, columns), BF16)],
    )(
        low, mid, high, own, combo, wide_t, wide, mine, theirs, proj_out, proj_t,
        taps_out, tile,
    )

    arrived = lax.all_to_all(sent, ("chan", "pipe"), 0, 0)
    near = 4
    far = slabs // near
    lines = share * 9 * part // columns
    sent = call(grad_kernel, shape((near, far, lines, columns), BF16), [VMEM] * 9)(
        arrived, slope, mine, theirs, grad, low, mid, high, proj_out
    )
    groups = [[near * i + j for j in range(near)] for i in range(far)]
    pieces = lax.all_to_all(sent, "slab", 0, 0, axis_index_groups=groups)
    partial = jnp.sum(pieces.astype(F32), axis=0).astype(BF16)
    groups = [[near * i + j for i in range(far)] for j in range(near)]
    pieces = lax.all_to_all(partial, "slab", 0, 0, axis_index_groups=groups)
    total = call(fold_kernel, shape((9, share, part), F32), [VMEM])(pieces)
    total = total.transpose(1, 0, 2)
    return out[None], total[None]


def solution(mesh):
    placed = (
        P("pipe", None, "slab", "chan", None),
        P("pipe", None, "chan"),
        P("pipe", None, None, None),
        P("pipe", None, None),
    )
    return jax.shard_map(
        on_device,
        mesh=mesh,
        in_specs=placed,
        out_specs=(P("pipe", None, "slab", "chan", None), P("pipe", "slab", None, "chan")),
        check_vma=False,
    )
```

```python
import functools
import math

import jax
import jax.numpy as jnp
from jax import lax
from jax.experimental import pallas as pl
from jax.experimental.pallas import tpu as pltpu
from jax.sharding import PartitionSpec as P

F32 = jnp.float32
BF16 = jnp.bfloat16
VMEM = pl.BlockSpec(memory_space=pltpu.VMEM)
HBM = pl.BlockSpec(memory_space=pltpu.HBM)


def dot(a, b):
    return lax.dot_general(a, b, (((1,), (0,)), ((), ())), preferred_element_type=F32)


def dot_nt(a, b):
    return lax.dot_general(a, b, (((1,), (1,)), ((), ())), preferred_element_type=F32)


def shifted(values, step):
    if step == 0:
        return values
    columns = values.shape[-1]
    lane = lax.broadcasted_iota(jnp.int32, values.shape, values.ndim - 1)
    edge = columns - 1 if step == 1 else 0
    moved = pltpu.roll(values, columns - 1 if step == 1 else 1, values.ndim - 1)
    return jnp.where(lane == edge, 0.0, moved)


def logistic(summed):
    return 0.5 + 0.5 * jnp.tanh(0.5 * summed)


def tap_blocks(rows, outs):
    sums = []
    for row in range(len(rows) - 2):
        total = None
        for col_tap in range(3):
            part = None
            for row_tap in range(3):
                at = (3 * row_tap + col_tap) * outs
                block = rows[row + row_tap][at : at + outs]
                part = block if part is None else part + block
            part = shifted(part, col_tap - 1)
            total = part if total is None else total + part
        sums.append(total)
    return sums


def block_of(pair, at, part):
    mine, theirs = pair
    count = mine.shape[0]
    rows = pl.ds(pl.multiple_of(at * part, part), part)
    left, right = mine[:, rows], theirs[:, rows]
    swap = lax.axis_index("chan") % 2 == 1
    even = jnp.where(swap, right, left)
    odd = jnp.where(swap, left, right)
    return jnp.concatenate([half[i] for i in range(count) for half in (even, odd)], axis=0)


def column(row):
    count = row.shape[1]
    square = jnp.broadcast_to(row, (count, count))
    line = lax.broadcasted_iota(jnp.int32, square.shape, 0)
    lane = lax.broadcasted_iota(jnp.int32, square.shape, 1)
    return jnp.sum(jnp.where(line == lane, square, 0.0), axis=1, keepdims=True)


def mix_weights(taps):
    encoder = lax.axis_index("pipe") == 0
    depth = [column(taps[lag : lag + 1].astype(F32)) for lag in range(3)]
    return [jnp.where(encoder, depth[lag], 1.0 if lag == 0 else 0.0) for lag in range(3)], depth


def mix_rows(history, weights):
    mixed = []
    for frame in range(len(history)):
        total = weights[0] * history[frame]
        for lag in range(1, 3):
            if frame >= lag:
                total = total + weights[lag] * history[frame - lag]
        mixed.append(total.astype(BF16))
    return mixed


def prepare_kernel(tile, taps, proj_t, mid, extra, direct, proj_out):
    frames, rows, part, columns = tile.shape
    latents = proj_t.shape[0]
    chan = lax.axis_index("chan")
    proj_back = pick(proj_t, chan, part)
    line = lax.broadcasted_iota(jnp.int32, (part, part), 0)
    lane = lax.broadcasted_iota(jnp.int32, (part, part), 1)
    turned = dot_nt(jnp.where(line == lane, 1.0, 0.0).astype(BF16), proj_back).astype(BF16)
    proj_out[...] = turned
    weights, depth = mix_weights(taps)
    line = lax.broadcasted_iota(jnp.int32, (latents, columns), 0)
    lane = lax.broadcasted_iota(jnp.int32, (latents, columns), 1)
    total = None
    for lag in range(3):
        spot = jnp.where(lane == line + lag * latents, 1.0, 0.0).astype(BF16)
        term = depth[lag] * dot(turned, spot)
        total = term if total is None else total + term
    extra[...] = total.astype(BF16)
    for row in range(rows):
        mixed = mix_rows([tile[frame, row].astype(F32) for frame in range(frames)], weights)
        for frame in range(frames):
            mid[frame, row] = mixed[frame]
            direct[frame * rows + row] = dot(proj_back, tile[frame, row]).astype(BF16)

def turn_kernel(after, kern, taps_out, held, done):
    columns = held.shape[2]
    part = taps_out.shape[0] // 9
    chan = lax.axis_index("chan")
    across = columns // part
    lanes = pl.ds(pl.multiple_of(chan // across * columns, columns), columns)
    fetch = pltpu.make_async_copy(kern.at[:, :, lanes], held, done)
    fetch.start()
    fetch.wait()
    for tap in range(9):
        block = held[tap].T
        chosen = block[:part]
        for at in range(1, across):
            chosen = jnp.where(chan % across == at, block[at * part : (at + 1) * part], chosen)
        taps_out[tap * part : (tap + 1) * part] = chosen


def mix_kernel(low, high, taps, mid, extra, direct, sent, own):
    frames, rows, part, columns = mid.shape
    chips = sent.shape[0]
    latents = direct.shape[1]
    weights, _ = mix_weights(taps)
    before = mix_rows([low[frame, rows - 1].astype(F32) for frame in range(frames)], weights)
    after = mix_rows([high[frame, 0].astype(F32) for frame in range(frames)], weights)
    for frame in range(frames):
        blocks = [before[frame]] + [mid[frame, row] for row in range(rows)] + [after[frame]]
        for row in range(rows + 2):
            own[frame, row] = blocks[row]
            at = (frame * (rows + 2) + row) * part
            for chip in range(chips):
                sent[chip, at : at + part] = blocks[row]
    at = frames * (rows + 2) * part
    encoder = lax.axis_index("pipe") == 0
    blank = jnp.zeros((part - latents, columns), BF16)
    for chip in range(chips):
        first = direct[min(chip, frames * rows - 1)]
        last = jnp.where(encoder, jnp.concatenate([first, blank], axis=0), extra[...])
        sent[chip, at : at + part] = last


def encode_kernel(
    mine, theirs, taps_out, proj_t, kern, sent, combo, wide_t, wide, *, frames, rows
):
    columns = mine.shape[2]
    gathered = (mine, theirs)
    part = taps_out.shape[0] // 9
    latents = proj_t.shape[0]
    deep = 3 * latents
    encoder, chan = lax.axis_index("pipe") == 0, lax.axis_index("chan")
    row_at, turn = chan // 2, chan % 2
    active = row_at < frames * rows

    @pl.when(jnp.logical_and(encoder, active))
    def _():
        base = (row_at // rows) * (rows + 2) + row_at % rows
        turned = [block_of(gathered, base + a, part).T for a in range(3)]
        summed = None
        for b in range(3):
            total = None
            for a in range(3):
                term = dot(turned[a], kern[3 * a + b])
                total = term if total is None else total + term
            if b != 1:
                line = lax.broadcasted_iota(jnp.int32, total.shape, 0)
                edge = columns - 1 if b == 2 else 0
                moved = pltpu.roll(total, columns - 1 if b == 2 else 1, 0)
                total = jnp.where(line == edge, 0.0, moved)
            summed = total if summed is None else summed + total
        bent = (summed * logistic(summed)).astype(BF16)
        latent = dot_nt(proj_t[...], bent)
        at = frames * (rows + 2) * part
        for chip in range(mine.shape[0]):
            for half in gathered:
                latent = latent + half[chip, at : at + latents].astype(F32)
        few = latents // 2
        latent = jnp.where(turn == 0, latent[:few], latent[few:]).astype(BF16)
        for peer in range(sent.shape[0]):
            sent[peer] = latent

    @pl.when(jnp.logical_not(jnp.logical_and(encoder, active)))
    def _():
        sent[...] = jnp.zeros_like(sent)

    @pl.when(jnp.logical_not(encoder))
    def _():
        factors = block_of(gathered, frames * (rows + 2), part)
        combo[...] = dot(taps_out[...], factors).astype(BF16)
        factors_t = factors.astype(F32).T.astype(BF16)[:deep]
        for tap in range(9):
            wide_t[tap * deep : (tap + 1) * deep] = dot(factors_t, kern[tap]).astype(BF16)
        wide[...] = wide_t[...].astype(F32).T.astype(BF16)


def pick(ref, turn, span):
    chosen = ref[:, :span]
    for at in range(1, ref.shape[1] // span):
        chosen = jnp.where(turn == at, ref[:, at * span : (at + 1) * span], chosen)
    return chosen


def stacked(z_rows, frame, frames):
    blank = jnp.zeros_like(z_rows[0])
    return jnp.concatenate(
        [z_rows[frame - lag] if frame >= lag else blank for lag in range(3)], axis=0
    )


def z_row(low, mid, high, frame, row):
    rows = mid.shape[1]
    if row < rows:
        return low[frame, row]
    if row < 2 * rows:
        return mid[frame, row - rows]
    return high[frame, row - 2 * rows]


def decode_kernel(
    scale, low, mid, high, own, combo, wide_t, wide, mine, theirs, proj_out, proj_t, taps_out, tile,
    out, slope, grad, sent, bank
):
    frames, rows, latents, columns = mid.shape
    outs = own.shape[2]
    part = outs
    deep = 3 * latents
    channels = wide.shape[0]
    gathered = (mine, theirs)
    encoder, chan = lax.axis_index("pipe") == 0, lax.axis_index("chan")
    row_at, turn = chan // 2, chan % 2
    active = row_at < frames * rows

    @pl.when(encoder)
    def _():
        weights = taps_out[...]
        for frame in range(frames):
            products = []
            for row in range(0, rows + 2, 2):
                at = frame * (rows + 2) + row
                pair = jnp.concatenate(
                    [block_of(gathered, at + k, part) for k in range(2)], axis=1
                )
                both = dot(weights, pair)
                products += [both[:, :columns], both[:, columns:]]
            for row, summed in enumerate(tap_blocks(products, outs)):
                sigma = logistic(summed)
                out[frame, row] = (tile[frame, row].astype(F32) + summed * sigma).astype(BF16)
                slope[frame, row] = sigma * (1.0 + summed * (1.0 - sigma))

    @pl.when(jnp.logical_or(encoder, jnp.logical_not(active)))
    def _():
        sent[...] = jnp.zeros_like(sent)

    @pl.when(jnp.logical_not(encoder))
    def _():
        weights = combo[...][:, :deep]
        reach = range(1, 3 * rows - 1)
        for frame in range(frames):
            band = jnp.concatenate(
                [
                    stacked(
                        [z_row(low, mid, high, f, row) for f in range(frames)], frame, frames
                    )
                    for row in reach
                ],
                axis=1,
            )
            both = dot(weights, band)
            products = [both[:, i * columns : (i + 1) * columns] for i in range(len(reach))]
            for row, summed in enumerate(tap_blocks(products, outs)):
                sigma = logistic(summed)
                cotangent = own[frame, row + 1].astype(F32) * scale
                bend = sigma * (1.0 + summed * (1.0 - sigma))
                grad[frame, row] = (cotangent * bend).astype(BF16)
                lifted = dot(proj_out[...], mid[frame, row]).astype(BF16)
                out[frame, row] = (lifted.astype(F32) + summed * sigma).astype(BF16)

    @pl.when(jnp.logical_and(jnp.logical_not(encoder), active))
    def _():
        bank[:, 0:2] = jnp.zeros((3, 2) + bank.shape[2:], BF16)
        for frame in range(frames):
            for row in range(3 * rows):
                value = z_row(low, mid, high, frame, row).astype(F32)
                for b in range(3):
                    bank[b, frame + 2, row] = shifted(value, b - 1).astype(BF16)
        frame_at, line = row_at // rows, row_at % rows
        def channel_rows(frame, row):
            return block_of(gathered, frame * (rows + 2) + row, part)

        columns_of = []
        for lag in range(3):
            source = jnp.minimum(frame_at + lag, frames - 1)
            for a in range(3):
                columns_of.append(
                    jnp.concatenate(
                        [
                            bank[tap % 3, source - back + 2, line - a + 2 + tap // 3]
                            for tap in range(9)
                            for back in range(3)
                        ],
                        axis=0,
                    )
                )
        summed = dot(wide[...], jnp.concatenate(columns_of, axis=1))
        slanted, weights = [], []
        for lag in range(3):
            source = jnp.minimum(frame_at + lag, frames - 1)
            factor = jnp.where(frame_at + lag < frames, scale, 0.0)
            for a in range(3):
                at = (3 * lag + a) * columns
                value = summed[:, at : at + columns]
                sigma = logistic(value)
                bend = sigma * (1.0 + value * (1.0 - sigma))
                cotangent = channel_rows(source, line - a + 2).astype(F32) * factor
                slanted.append((cotangent * bend).astype(BF16))
                weights.append(
                    jnp.concatenate(
                        [
                            wide_t[(3 * a + b) * deep + lag * latents :][:latents]
                            for b in range(3)
                        ],
                        axis=0,
                    )
                )
        mixed = dot(jnp.concatenate(weights, axis=1), jnp.concatenate(slanted, axis=0))
        latent = dot(proj_t[...], channel_rows(frame_at, line + 1)) * scale
        for b in range(3):
            latent = latent + shifted(mixed[b * latents : (b + 1) * latents], 1 - b)
        few = latents // 2
        latent = jnp.where(turn == 0, latent[:few], latent[few:]).astype(BF16)
        for peer in range(sent.shape[0]):
            sent[peer] = latent


def grad_kernel(
    arrived, slope, mine, theirs, grad, low, mid, high, proj_out, sent
):
    frames, rows, outs, columns = slope.shape
    gathered = (mine, theirs)
    part = outs
    near, far = sent.shape[:2]
    share = 2 * mine.shape[0] * part // (near * far)
    latents = mid.shape[2]
    encoder = lax.axis_index("pipe") == 0

    def window(grads, frame, row):
        blank = jnp.zeros((outs, columns), BF16)
        return jnp.concatenate(
            [
                grads[frame][row - a][b] if 0 <= row - a < rows else blank
                for a in range(3)
                for b in range(3)
            ],
            axis=0,
        )

    def steps(value):
        return [shifted(value.astype(F32), 1 - b).astype(BF16) for b in range(3)]

    def store(total):
        total = total.astype(BF16).astype(F32)
        wide = (9 * outs // columns) * columns
        folds = columns // (9 * outs - wide)
        few = share // folds
        for i in range(far):
            for j in range(near):
                at = (near * i + j) * share
                block = total[at : at + share]
                pieces = [block[:, k : k + columns] for k in range(0, wide, columns)]
                rest = [block[k * few : (k + 1) * few, wide:] for k in range(folds)]
                pieces.append(jnp.concatenate(rest, axis=1))
                sent[j, i] = jnp.concatenate(pieces, axis=0).astype(BF16)

    spots = [(frame, row) for frame in range(frames) for row in range(rows + 2)]

    @pl.when(encoder)
    def _():
        grads = []
        for frame in range(frames):
            grads.append([])
            for row in range(rows):
                at = 4 * (frame * rows + row)
                latent = jnp.concatenate(
                    [arrived[at + 1].astype(F32), arrived[at + 3].astype(F32)], axis=0
                )
                value = dot(proj_out[...], latent.astype(BF16)) * slope[frame, row]
                grads[-1].append(steps(value.astype(BF16)))
        left = jnp.concatenate(
            [block_of(gathered, at, part) for at in range(len(spots))], axis=1
        )
        right = jnp.concatenate([window(grads, frame, row) for frame, row in spots], axis=1)
        store(dot_nt(left, right))

    @pl.when(jnp.logical_not(encoder))
    def _():
        grads = [[steps(grad[frame, row]) for row in range(rows)] for frame in range(frames)]
        left = jnp.concatenate(
            [
                stacked(
                    [z_row(low, mid, high, f, row + 1) for f in range(frames)], frame, frames
                )
                for frame, row in spots
            ],
            axis=1,
        )
        right = jnp.concatenate([window(grads, frame, row) for frame, row in spots], axis=1)
        inner = dot_nt(left, right).astype(BF16)
        factors = block_of(gathered, len(spots), part)
        store(dot(factors[:, : 3 * latents], inner))


def fold_kernel(pieces, out):
    taps, share, outs = out.shape
    columns = pieces.shape[2]
    total = pieces[0].astype(F32)
    for pair in range(1, pieces.shape[0]):
        total = total + pieces[pair].astype(F32)
    across = columns // outs
    for tap in range(taps - 1):
        at = tap // across * share
        lane = tap % across * outs
        out[tap] = total[at : at + share, lane : lane + outs]
    rest = total[(taps - 1) // across * share :]
    out[taps - 1] = jnp.concatenate(
        [rest[:, i * outs : (i + 1) * outs] for i in range(across)], axis=0
    )


def call(kernel, shapes, specs, scratch=(), limit=40):
    return pl.pallas_call(
        kernel,
        out_shape=shapes,
        in_specs=specs,
        out_specs=jax.tree.map(lambda _: VMEM, shapes),
        scratch_shapes=list(scratch),
        compiler_params=pltpu.CompilerParams(vmem_limit_bytes=limit * 1024 * 1024),
    )


def both_ways(low_side, high_side, axis):
    count = lax.axis_size(axis)
    forward = [(i, i + 1) for i in range(count - 1)]
    backward = [(i + 1, i) for i in range(count - 1)]
    return lax.ppermute(high_side, axis, forward), lax.ppermute(low_side, axis, backward)


def on_device(features, taps, kern, proj):
    shape = jax.ShapeDtypeStruct
    peers = lax.axis_size("chan")
    slabs = lax.axis_size("slab")
    both = peers * lax.axis_size("pipe")
    tile = features[0]
    frames, rows, part, columns = tile.shape
    channels, latents = proj.shape[1], proj.shape[2]
    share = channels // slabs
    scale = 1.0 / math.sqrt(frames * rows * slabs * columns)
    by_tap = kern[0].transpose(1, 0, 2)

    above, below = both_ways(tile, tile, "slab")
    proj_t = proj[0].T
    height = (frames * (rows + 2) + 1) * part
    middle, extra, direct, proj_out = call(
        prepare_kernel,
        (
            shape(tile.shape, BF16),
            shape((part, columns), BF16),
            shape((frames * rows, latents, columns), BF16),
            shape((part, latents), BF16),
        ),
        [VMEM] * 3,
    )(tile, taps[0], proj_t)
    sent, own = call(
        mix_kernel,
        (
            shape((peers // 2, height, columns), BF16),
            shape((frames, rows + 2, part, columns), BF16),
        ),
        [VMEM] * 6,
    )(above, below, taps[0], middle, extra, direct)
    groups = [[2 * chip + core for chip in range(peers // 2)] for core in range(2)]
    mine = lax.all_to_all(sent, "chan", 0, 0, axis_index_groups=groups)
    theirs = lax.ppermute(mine, "chan", [(i, i ^ 1) for i in range(peers)])

    taps_out = call(
        turn_kernel,
        shape((9 * part, channels), BF16),
        [HBM] * 2,
        [pltpu.VMEM((9, channels, columns), BF16), pltpu.SemaphoreType.DMA],
        limit=51,
    )(mine, by_tap)
    tile_shape = (frames, rows, part, columns)
    latent_shape = (both, latents // 2, columns)
    terms = 27 * latents
    sent, combo, wide_t, wide = call(
        functools.partial(encode_kernel, frames=frames, rows=rows),
        (
            shape(latent_shape, BF16),
            shape((9 * part, columns), BF16),
            shape((terms, channels), BF16),
            shape((channels, terms), BF16),
        ),
        [VMEM] * 5,
    )(mine, theirs, taps_out, proj_t, by_tap)

    arrived = lax.all_to_all(sent, ("chan", "pipe"), 0, 0)
    arrived = arrived.reshape(peers, 2, latents // 2, columns)[: frames * rows * 2, 0]
    mid = arrived.reshape(frames, rows, latents, columns)
    low, high = both_ways(mid, mid, "slab")
    out, slope, grad, sent = call(
        functools.partial(decode_kernel, scale),
        (
            shape(tile_shape, BF16),
            shape(tile_shape, F32),
            shape(tile_shape, BF16),
            shape(latent_shape, BF16),
        ),
        [VMEM] * 13,
        [pltpu.VMEM((3, frames + 2, 3 * rows, latents, columns), BF16)],
    )(
        low, mid, high, own, combo, wide_t, wide, mine, theirs, proj_out, proj_t,
        taps_out, tile,
    )

    arrived = lax.all_to_all(sent, ("chan", "pipe"), 0, 0)
    near = 4
    far = slabs // near
    lines = share * 9 * part // columns
    sent = call(grad_kernel, shape((near, far, lines, columns), BF16), [VMEM] * 9)(
        arrived, slope, mine, theirs, grad, low, mid, high, proj_out
    )
    groups = [[near * i + j for j in range(near)] for i in range(far)]
    pieces = lax.all_to_all(sent, "slab", 0, 0, axis_index_groups=groups)
    partial = jnp.sum(pieces.astype(F32), axis=0).astype(BF16)
    groups = [[near * i + j for i in range(far)] for j in range(near)]
    pieces = lax.all_to_all(partial, "slab", 0, 0, axis_index_groups=groups)
    total = call(fold_kernel, shape((9, share, part), F32), [VMEM])(pieces)
    total = total.transpose(1, 0, 2)
    return out[None], total[None]


def solution(mesh):
    placed = (
        P("pipe", None, "slab", "chan", None),
        P("pipe", None, "chan"),
        P("pipe", None, None, None),
        P("pipe", None, None),
    )
    return jax.shard_map(
        on_device,
        mesh=mesh,
        in_specs=placed,
        out_specs=(P("pipe", None, "slab", "chan", None), P("pipe", "slab", None, "chan")),
        check_vma=False,
    )
```

```python
import functools
import math

import jax
import jax.numpy as jnp
from jax import lax
from jax.experimental import pallas as pl
from jax.experimental.pallas import tpu as pltpu
from jax.sharding import PartitionSpec as P

F32 = jnp.float32
BF16 = jnp.bfloat16
VMEM = pl.BlockSpec(memory_space=pltpu.VMEM)
HBM = pl.BlockSpec(memory_space=pltpu.HBM)


def dot(a, b):
    return lax.dot_general(a, b, (((1,), (0,)), ((), ())), preferred_element_type=F32)


def dot_nt(a, b):
    return lax.dot_general(a, b, (((1,), (1,)), ((), ())), preferred_element_type=F32)


def shifted(values, step):
    if step == 0:
        return values
    columns = values.shape[-1]
    lane = lax.broadcasted_iota(jnp.int32, values.shape, values.ndim - 1)
    edge = columns - 1 if step == 1 else 0
    moved = pltpu.roll(values, columns - 1 if step == 1 else 1, values.ndim - 1)
    return jnp.where(lane == edge, 0.0, moved)


def logistic(summed):
    return 1.0 / (1.0 + jnp.exp(-summed))


def tap_blocks(rows, outs):
    sums = []
    for row in range(len(rows) - 2):
        total = None
        for col_tap in range(3):
            part = None
            for row_tap in range(3):
                at = (3 * row_tap + col_tap) * outs
                block = rows[row + row_tap][at : at + outs]
                part = block if part is None else part + block
            part = shifted(part, col_tap - 1)
            total = part if total is None else total + part
        sums.append(total)
    return sums


def block_of(pair, at, part):
    mine, theirs = pair
    count = mine.shape[0]
    rows = pl.ds(pl.multiple_of(at * part, part), part)
    left, right = mine[:, rows], theirs[:, rows]
    swap = lax.axis_index("chan") % 2 == 1
    even = jnp.where(swap, right, left)
    odd = jnp.where(swap, left, right)
    return jnp.concatenate([half[i] for i in range(count) for half in (even, odd)], axis=0)


def column(row):
    count = row.shape[1]
    square = jnp.broadcast_to(row, (count, count))
    line = lax.broadcasted_iota(jnp.int32, square.shape, 0)
    lane = lax.broadcasted_iota(jnp.int32, square.shape, 1)
    return jnp.sum(jnp.where(line == lane, square, 0.0), axis=1, keepdims=True)


def mix_weights(taps):
    encoder = lax.axis_index("pipe") == 0
    depth = [column(taps[lag : lag + 1].astype(F32)) for lag in range(3)]
    return [jnp.where(encoder, depth[lag], 1.0 if lag == 0 else 0.0) for lag in range(3)], depth


def mix_rows(history, weights):
    mixed = []
    for frame in range(len(history)):
        total = weights[0] * history[frame]
        for lag in range(1, 3):
            if frame >= lag:
                total = total + weights[lag] * history[frame - lag]
        mixed.append(total.astype(BF16))
    return mixed


def prepare_kernel(tile, small, mid, extra, direct, proj_out):
    frames, rows, part, columns = tile.shape
    latents = direct.shape[1]
    proj_t, taps = small[:latents], small[latents:][:3, :part]
    chan = lax.axis_index("chan")
    proj_back = pick(proj_t, chan, part)
    line = lax.broadcasted_iota(jnp.int32, (part, part), 0)
    lane = lax.broadcasted_iota(jnp.int32, (part, part), 1)
    turned = dot_nt(jnp.where(line == lane, 1.0, 0.0).astype(BF16), proj_back).astype(BF16)
    proj_out[...] = turned
    weights, depth = mix_weights(taps)
    line = lax.broadcasted_iota(jnp.int32, (latents, columns), 0)
    lane = lax.broadcasted_iota(jnp.int32, (latents, columns), 1)
    total = None
    for lag in range(3):
        spot = jnp.where(lane == line + lag * latents, 1.0, 0.0).astype(BF16)
        term = depth[lag] * dot(turned, spot)
        total = term if total is None else total + term
    extra[...] = total.astype(BF16)
    for row in range(rows):
        mixed = mix_rows([tile[frame, row].astype(F32) for frame in range(frames)], weights)
        for frame in range(frames):
            mid[frame, row] = mixed[frame]
            direct[frame * rows + row] = dot(proj_back, tile[frame, row]).astype(BF16)

def turn_kernel(after, kern, taps_out, held, done):
    columns = held.shape[2]
    part = taps_out.shape[0] // 9
    chan = lax.axis_index("chan")
    across = columns // part
    lanes = pl.ds(pl.multiple_of(chan // across * columns, columns), columns)
    fetch = pltpu.make_async_copy(kern.at[:, :, lanes], held, done)
    fetch.start()
    fetch.wait()
    for tap in range(9):
        block = held[tap].T
        chosen = block[:part]
        for at in range(1, across):
            chosen = jnp.where(chan % across == at, block[at * part : (at + 1) * part], chosen)
        taps_out[tap * part : (tap + 1) * part] = chosen


def mix_kernel(low, high, small, mid, extra, direct, sent, own):
    frames, rows, part, columns = mid.shape
    chips = sent.shape[0]
    latents = direct.shape[1]
    taps = small[latents:][:3, :part]
    weights, _ = mix_weights(taps)
    before = mix_rows([low[frame, rows - 1].astype(F32) for frame in range(frames)], weights)
    after = mix_rows([high[frame, 0].astype(F32) for frame in range(frames)], weights)
    for frame in range(frames):
        blocks = [before[frame]] + [mid[frame, row] for row in range(rows)] + [after[frame]]
        for row in range(rows + 2):
            own[frame, row] = blocks[row]
            at = (frame * (rows + 2) + row) * part
            for chip in range(chips):
                sent[chip, at : at + part] = blocks[row]
    at = frames * (rows + 2) * part
    encoder = lax.axis_index("pipe") == 0
    blank = jnp.zeros((part - latents, columns), BF16)
    for chip in range(chips):
        first = direct[min(chip, frames * rows - 1)]
        last = jnp.where(encoder, jnp.concatenate([first, blank], axis=0), extra[...])
        sent[chip, at : at + part] = last


def encode_kernel(
    mine, theirs, taps_out, proj_t, kern, sent, combo, wide_t, wide, *, frames, rows
):
    columns = mine.shape[2]
    gathered = (mine, theirs)
    part = taps_out.shape[0] // 9
    latents = proj_t.shape[0]
    deep = 3 * latents
    encoder, chan = lax.axis_index("pipe") == 0, lax.axis_index("chan")
    row_at, turn = chan // 2, chan % 2
    active = row_at < frames * rows

    @pl.when(jnp.logical_and(encoder, active))
    def _():
        base = (row_at // rows) * (rows + 2) + row_at % rows
        turned = [block_of(gathered, base + a, part).T for a in range(3)]
        summed = None
        for b in range(3):
            total = None
            for a in range(3):
                term = dot(turned[a], kern[3 * a + b])
                total = term if total is None else total + term
            if b != 1:
                line = lax.broadcasted_iota(jnp.int32, total.shape, 0)
                edge = columns - 1 if b == 2 else 0
                moved = pltpu.roll(total, columns - 1 if b == 2 else 1, 0)
                total = jnp.where(line == edge, 0.0, moved)
            summed = total if summed is None else summed + total
        bent = (summed * logistic(summed)).astype(BF16)
        latent = dot_nt(proj_t[...], bent)
        at = frames * (rows + 2) * part
        for chip in range(mine.shape[0]):
            for half in gathered:
                latent = latent + half[chip, at : at + latents].astype(F32)
        few = latents // 2
        latent = jnp.where(turn == 0, latent[:few], latent[few:]).astype(BF16)
        for peer in range(sent.shape[0]):
            sent[peer] = latent

    @pl.when(jnp.logical_not(jnp.logical_and(encoder, active)))
    def _():
        sent[...] = jnp.zeros_like(sent)

    @pl.when(jnp.logical_not(encoder))
    def _():
        factors = block_of(gathered, frames * (rows + 2), part)
        combo[...] = dot(taps_out[...], factors).astype(BF16)
        factors_t = factors.astype(F32).T.astype(BF16)[:deep]
        for tap in range(9):
            wide_t[tap * deep : (tap + 1) * deep] = dot(factors_t, kern[tap]).astype(BF16)
        wide[...] = wide_t[...].astype(F32).T.astype(BF16)


def pick(ref, turn, span):
    chosen = ref[:, :span]
    for at in range(1, ref.shape[1] // span):
        chosen = jnp.where(turn == at, ref[:, at * span : (at + 1) * span], chosen)
    return chosen


def stacked(z_rows, frame, frames):
    blank = jnp.zeros_like(z_rows[0])
    return jnp.concatenate(
        [z_rows[frame - lag] if frame >= lag else blank for lag in range(3)], axis=0
    )


def z_row(low, mid, high, frame, row):
    rows = mid.shape[1]
    if row < rows:
        return low[frame, row]
    if row < 2 * rows:
        return mid[frame, row - rows]
    return high[frame, row - 2 * rows]


def decode_kernel(
    scale, low, mid, high, own, combo, wide_t, wide, mine, theirs, proj_out, proj_t, taps_out, tile,
    out, slope, grad, sent, bank
):
    frames, rows, latents, columns = mid.shape
    outs = own.shape[2]
    part = outs
    deep = 3 * latents
    channels = wide.shape[0]
    gathered = (mine, theirs)
    encoder, chan = lax.axis_index("pipe") == 0, lax.axis_index("chan")
    row_at, turn = chan // 2, chan % 2
    active = row_at < frames * rows

    @pl.when(encoder)
    def _():
        weights = taps_out[...]
        for frame in range(frames):
            products = []
            for row in range(0, rows + 2, 2):
                at = frame * (rows + 2) + row
                pair = jnp.concatenate(
                    [block_of(gathered, at + k, part) for k in range(2)], axis=1
                )
                both = dot(weights, pair)
                products += [both[:, :columns], both[:, columns:]]
            for row, summed in enumerate(tap_blocks(products, outs)):
                sigma = logistic(summed)
                out[frame, row] = (tile[frame, row].astype(F32) + summed * sigma).astype(BF16)
                slope[frame, row] = sigma * (1.0 + summed * (1.0 - sigma))

    @pl.when(jnp.logical_or(encoder, jnp.logical_not(active)))
    def _():
        sent[...] = jnp.zeros_like(sent)

    @pl.when(jnp.logical_not(encoder))
    def _():
        weights = combo[...][:, :deep]
        reach = range(1, 3 * rows - 1)
        for frame in range(frames):
            band = jnp.concatenate(
                [
                    stacked(
                        [z_row(low, mid, high, f, row) for f in range(frames)], frame, frames
                    )
                    for row in reach
                ],
                axis=1,
            )
            both = dot(weights, band)
            products = [both[:, i * columns : (i + 1) * columns] for i in range(len(reach))]
            for row, summed in enumerate(tap_blocks(products, outs)):
                sigma = logistic(summed)
                cotangent = own[frame, row + 1].astype(F32) * scale
                bend = sigma * (1.0 + summed * (1.0 - sigma))
                grad[frame, row] = (cotangent * bend).astype(BF16)
                lifted = dot(proj_out[...], mid[frame, row]).astype(BF16)
                out[frame, row] = (lifted.astype(F32) + summed * sigma).astype(BF16)

    @pl.when(jnp.logical_and(jnp.logical_not(encoder), active))
    def _():
        bank[:, 0:2] = jnp.zeros((3, 2) + bank.shape[2:], BF16)
        for frame in range(frames):
            for row in range(3 * rows):
                value = z_row(low, mid, high, frame, row).astype(F32)
                for b in range(3):
                    bank[b, frame + 2, row] = shifted(value, b - 1).astype(BF16)
        frame_at, line = row_at // rows, row_at % rows
        def channel_rows(frame, row):
            return block_of(gathered, frame * (rows + 2) + row, part)

        columns_of = []
        for lag in range(3):
            source = jnp.minimum(frame_at + lag, frames - 1)
            for a in range(3):
                columns_of.append(
                    jnp.concatenate(
                        [
                            bank[tap % 3, source - back + 2, line - a + 2 + tap // 3]
                            for tap in range(9)
                            for back in range(3)
                        ],
                        axis=0,
                    )
                )
        summed = dot(wide[...], jnp.concatenate(columns_of, axis=1))
        slanted, weights = [], []
        for lag in range(3):
            source = jnp.minimum(frame_at + lag, frames - 1)
            factor = jnp.where(frame_at + lag < frames, scale, 0.0)
            for a in range(3):
                at = (3 * lag + a) * columns
                value = summed[:, at : at + columns]
                sigma = logistic(value)
                bend = sigma * (1.0 + value * (1.0 - sigma))
                cotangent = channel_rows(source, line - a + 2).astype(F32) * factor
                slanted.append((cotangent * bend).astype(BF16))
                weights.append(
                    jnp.concatenate(
                        [
                            wide_t[(3 * a + b) * deep + lag * latents :][:latents]
                            for b in range(3)
                        ],
                        axis=0,
                    )
                )
        mixed = dot(jnp.concatenate(weights, axis=1), jnp.concatenate(slanted, axis=0))
        latent = dot(proj_t[...], channel_rows(frame_at, line + 1)) * scale
        for b in range(3):
            latent = latent + shifted(mixed[b * latents : (b + 1) * latents], 1 - b)
        few = latents // 2
        latent = jnp.where(turn == 0, latent[:few], latent[few:]).astype(BF16)
        for peer in range(sent.shape[0]):
            sent[peer] = latent


def grad_kernel(
    arrived, slope, mine, theirs, grad, low, mid, high, proj_out, sent
):
    frames, rows, outs, columns = slope.shape
    gathered = (mine, theirs)
    part = outs
    near, far = sent.shape[:2]
    share = 2 * mine.shape[0] * part // (near * far)
    latents = mid.shape[2]
    encoder = lax.axis_index("pipe") == 0

    def window(grads, frame, row):
        blank = jnp.zeros((outs, columns), BF16)
        return jnp.concatenate(
            [
                grads[frame][row - a][b] if 0 <= row - a < rows else blank
                for a in range(3)
                for b in range(3)
            ],
            axis=0,
        )

    def steps(value):
        return [shifted(value.astype(F32), 1 - b).astype(BF16) for b in range(3)]

    def store(total):
        total = total.astype(BF16).astype(F32)
        wide = (9 * outs // columns) * columns
        folds = columns // (9 * outs - wide)
        few = share // folds
        for i in range(far):
            for j in range(near):
                at = (near * i + j) * share
                block = total[at : at + share]
                pieces = [block[:, k : k + columns] for k in range(0, wide, columns)]
                rest = [block[k * few : (k + 1) * few, wide:] for k in range(folds)]
                pieces.append(jnp.concatenate(rest, axis=1))
                sent[j, i] = jnp.concatenate(pieces, axis=0).astype(BF16)

    spots = [(frame, row) for frame in range(frames) for row in range(rows + 2)]

    @pl.when(encoder)
    def _():
        grads = []
        for frame in range(frames):
            grads.append([])
            for row in range(rows):
                at = 4 * (frame * rows + row)
                latent = jnp.concatenate(
                    [arrived[at + 1].astype(F32), arrived[at + 3].astype(F32)], axis=0
                )
                value = dot(proj_out[...], latent.astype(BF16)) * slope[frame, row]
                grads[-1].append(steps(value.astype(BF16)))
        left = jnp.concatenate(
            [block_of(gathered, at, part) for at in range(len(spots))], axis=1
        )
        right = jnp.concatenate([window(grads, frame, row) for frame, row in spots], axis=1)
        store(dot_nt(left, right))

    @pl.when(jnp.logical_not(encoder))
    def _():
        grads = [[steps(grad[frame, row]) for row in range(rows)] for frame in range(frames)]
        left = jnp.concatenate(
            [
                stacked(
                    [z_row(low, mid, high, f, row + 1) for f in range(frames)], frame, frames
                )
                for frame, row in spots
            ],
            axis=1,
        )
        right = jnp.concatenate([window(grads, frame, row) for frame, row in spots], axis=1)
        inner = dot_nt(left, right).astype(BF16)
        factors = block_of(gathered, len(spots), part)
        store(dot(factors[:, : 3 * latents], inner))


def fold_kernel(pieces, out):
    taps, share, outs = out.shape
    columns = pieces.shape[2]
    total = pieces[0].astype(F32)
    for pair in range(1, pieces.shape[0]):
        total = total + pieces[pair].astype(F32)
    across = columns // outs
    for tap in range(taps - 1):
        at = tap // across * share
        lane = tap % across * outs
        out[tap] = total[at : at + share, lane : lane + outs]
    rest = total[(taps - 1) // across * share :]
    out[taps - 1] = jnp.concatenate(
        [rest[:, i * outs : (i + 1) * outs] for i in range(across)], axis=0
    )


def call(kernel, shapes, specs, scratch=(), limit=40):
    return pl.pallas_call(
        kernel,
        out_shape=shapes,
        in_specs=specs,
        out_specs=jax.tree.map(lambda _: VMEM, shapes),
        scratch_shapes=list(scratch),
        compiler_params=pltpu.CompilerParams(vmem_limit_bytes=limit * 1024 * 1024),
    )


def both_ways(low_side, high_side, axis):
    count = lax.axis_size(axis)
    forward = [(i, i + 1) for i in range(count - 1)]
    backward = [(i + 1, i) for i in range(count - 1)]
    return lax.ppermute(high_side, axis, forward), lax.ppermute(low_side, axis, backward)


def on_device(features, taps, kern, proj):
    shape = jax.ShapeDtypeStruct
    peers = lax.axis_size("chan")
    slabs = lax.axis_size("slab")
    both = peers * lax.axis_size("pipe")
    tile = features[0]
    frames, rows, part, columns = tile.shape
    channels, latents = proj.shape[1], proj.shape[2]
    share = channels // slabs
    scale = 1.0 / math.sqrt(frames * rows * slabs * columns)
    by_tap = kern[0].transpose(1, 0, 2)

    above, below = both_ways(tile, tile, "slab")
    proj_t = proj[0].T
    wide_taps = jnp.pad(taps[0], ((0, latents - 3), (0, channels - part)))
    small = jnp.concatenate([proj_t, wide_taps], axis=0)
    height = (frames * (rows + 2) + 1) * part
    middle, extra, direct, proj_out = call(
        prepare_kernel,
        (
            shape(tile.shape, BF16),
            shape((part, columns), BF16),
            shape((frames * rows, latents, columns), BF16),
            shape((part, latents), BF16),
        ),
        [VMEM] * 2,
    )(tile, small)
    sent, own = call(
        mix_kernel,
        (
            shape((peers // 2, height, columns), BF16),
            shape((frames, rows + 2, part, columns), BF16),
        ),
        [VMEM] * 6,
    )(above, below, small, middle, extra, direct)
    groups = [[2 * chip + core for chip in range(peers // 2)] for core in range(2)]
    mine = lax.all_to_all(sent, "chan", 0, 0, axis_index_groups=groups)
    theirs = lax.ppermute(mine, "chan", [(i, i ^ 1) for i in range(peers)])

    taps_out = call(
        turn_kernel,
        shape((9 * part, channels), BF16),
        [HBM] * 2,
        [pltpu.VMEM((9, channels, columns), BF16), pltpu.SemaphoreType.DMA],
        limit=51,
    )(mine, by_tap)
    tile_shape = (frames, rows, part, columns)
    latent_shape = (both, latents // 2, columns)
    terms = 27 * latents
    sent, combo, wide_t, wide = call(
        functools.partial(encode_kernel, frames=frames, rows=rows),
        (
            shape(latent_shape, BF16),
            shape((9 * part, columns), BF16),
            shape((terms, channels), BF16),
            shape((channels, terms), BF16),
        ),
        [VMEM] * 5,
    )(mine, theirs, taps_out, proj_t, by_tap)

    arrived = lax.all_to_all(sent, ("chan", "pipe"), 0, 0)
    arrived = arrived.reshape(peers, 2, latents // 2, columns)[: frames * rows * 2, 0]
    mid = arrived.reshape(frames, rows, latents, columns)
    low, high = both_ways(mid, mid, "slab")
    out, slope, grad, sent = call(
        functools.partial(decode_kernel, scale),
        (
            shape(tile_shape, BF16),
            shape(tile_shape, F32),
            shape(tile_shape, BF16),
            shape(latent_shape, BF16),
        ),
        [VMEM] * 13,
        [pltpu.VMEM((3, frames + 2, 3 * rows, latents, columns), BF16)],
    )(
        low, mid, high, own, combo, wide_t, wide, mine, theirs, proj_out, proj_t,
        taps_out, tile,
    )

    arrived = lax.all_to_all(sent, ("chan", "pipe"), 0, 0)
    near = 4
    far = slabs // near
    lines = share * 9 * part // columns
    sent = call(grad_kernel, shape((near, far, lines, columns), BF16), [VMEM] * 9)(
        arrived, slope, mine, theirs, grad, low, mid, high, proj_out
    )
    groups = [[near * i + j for j in range(near)] for i in range(far)]
    pieces = lax.all_to_all(sent, "slab", 0, 0, axis_index_groups=groups)
    partial = jnp.sum(pieces.astype(F32), axis=0).astype(BF16)
    groups = [[near * i + j for i in range(far)] for j in range(near)]
    pieces = lax.all_to_all(partial, "slab", 0, 0, axis_index_groups=groups)
    total = call(fold_kernel, shape((9, share, part), F32), [VMEM])(pieces)
    total = total.transpose(1, 0, 2)
    return out[None], total[None]


def solution(mesh):
    placed = (
        P("pipe", None, "slab", "chan", None),
        P("pipe", None, "chan"),
        P("pipe", None, None, None),
        P("pipe", None, None),
    )
    return jax.shard_map(
        on_device,
        mesh=mesh,
        in_specs=placed,
        out_specs=(P("pipe", None, "slab", "chan", None), P("pipe", "slab", None, "chan")),
        check_vma=False,
    )
```
